256 devices in a mesh: hst: 32 (over y, z_hi, x), local: 8 (over z_lo, core).
Axes of the slice: x: 4, y: 4, z: 8 (z_hi: 2, z_lo: 4; z = z_hi * 4 + z_lo), core: 2. Of those that a mesh axis runs over, the one named last changes fastest.
Arguments:
- pooled: bfloat16 [32768, 64, 128], P(('hst', 'local')), may hold values from -6 to 6
- cotangent: bfloat16 [32768, 64, 128], P(('hst', 'local')), may hold values from -6 to 6
- projection: bfloat16 [64, 16], replicated, may hold values from -0.75 to 0.75
- w_up: bfloat16 [1024, 512], replicated, may hold values from -0.1875 to 0.1875
- w_down: bfloat16 [512, 4096], replicated, may hold values from -0.25 to 0.25
- w_compress: bfloat16 [32, 64], replicated, may hold values from -0.75 to 0.75
- ln_gain: float32 [128], replicated, may hold values from 0.5 to 1.5
- feature_map: int32 [64], replicated, may hold values from 0 to 63, each once
- bag_row_index: int32 [32768, 64, 2], P(('hst', 'local')), may hold values from 0 to 4095
Outputs:
- table_grad: float32 [64, 4096, 128], P('hst', 'local')
- grad_w_up: float32 [1024, 512], P(('hst', 'local'))
- grad_w_down: float32 [512, 4096], P(('hst', 'local'))
- grad_projection: float32 [64, 16], replicated
- compress_weight_gradient: float32 [32, 64], replicated
- grad_gain: float32 [128], replicated
The draws below stay inside these ranges and needn't reach their ends.
Inputs may be any that keep to these rules, and one draw needn't show every extreme that they name: feature_map names every feature once.
All inputs are finite; a program needn't handle non-finite values.
Results may differ from the reference program's by a relative error of at most 0.0095.
Values may be sent and summed in bfloat16 or wider, within the bound.
No kernel may reach another device: no remote copies, remote signals or barrier semaphores. Data moves between devices by JAX's collectives and lax.ppermute only.
A program may use at most 128 MiB of HBM per device.

```python
import math
import jax
import jax.numpy as jnp
import numpy as np
from jax import lax

NF = 64
E = 128
K = 16
H = 512
L = 2
NF_F = 32
NF_L = 32
SAMPLES = 32768
ROWS = 4096


def with_ends(drawn, own_key, low, high):
    shape = drawn.shape
    spot = [jax.random.randint(jax.random.fold_in(own_key, axis), (), 0, shape[axis]) for axis in range(len(shape))]
    drawn = drawn.at[tuple(spot)].set(low)
    longest = shape.index(max(shape))
    spot[longest] = (spot[longest] + 1) % shape[longest]
    return drawn.at[tuple(spot)].set(high)


def level_of(key, shape, split, smallest, high):
    level, own = 1.0, jax.random.fold_in(key, 6)
    for dim, blocks in split:
        heights = jnp.exp(jax.random.uniform(jax.random.fold_in(own, dim), (blocks,), jnp.float32, smallest / len(split), high / len(split)))
        level = level * jnp.repeat(heights, shape[dim] // blocks).reshape([-1 if axis == dim else 1 for axis in range(len(shape))])
    return level


def cumulative_ranks(amount, skew):
    weights = [(1 << 20) // math.isqrt(rank ** skew) + 1 for rank in range(1, amount + 1)]
    width = 1 + sum(weights) // (1 << 30)
    return np.cumsum(np.array([max(1, weight // width) for weight in weights]))


def skewed_ids(stream_key, dims, amount, slope):
    table = cumulative_ranks(amount, slope)
    pick = jax.random.randint(jax.random.fold_in(stream_key, 1), dims, 0, int(table[amount - 1]))
    grade = jnp.searchsorted(jnp.asarray(table, jnp.int32), pick, side="right")
    return jax.random.permutation(jax.random.fold_in(stream_key, 2), amount)[grade].astype(jnp.int32)


def scatter_about(own_key, extent, deviation, reach, shards=(), kind=jnp.bfloat16):
    entries = jax.random.normal(own_key, extent, jnp.float32) * deviation
    if len(shards) > 0:
        entries = level_of(own_key, extent, shards, -0.22, 0.18) * entries
    return jnp.clip(entries, min=-reach, max=reach).astype(kind)


def setup_inputs(seed: int = 0) -> dict:
    key_list = jax.random.split(jax.random.key(seed), 10)
    pooled = scatter_about(key_list[0], (SAMPLES, NF, E), 1.0, 6.0, ((0, 256),))
    cotangent = scatter_about(key_list[1], (SAMPLES, NF, E), 1.0, 6.0, ((0, 256),))
    projection = scatter_about(key_list[2], (NF, K), NF ** -0.5, 0.75)
    w_up = scatter_about(key_list[3], (NF * K, H), (NF * K) ** -0.5, 0.1875)
    w_down = scatter_about(key_list[4], (H, NF_F * E), H ** -0.5, 0.25)
    w_compress = scatter_about(key_list[5], (NF_L, NF), NF ** -0.5, 0.75)
    ln_gain = jnp.clip(1.0 + 0.1 * jax.random.normal(key_list[6], (E,), jnp.float32), 0.5, 1.5)
    feature_map = jax.random.permutation(key_list[7], NF).astype(jnp.int32)
    bag_row_index = with_ends(skewed_ids(key_list[8], (SAMPLES, NF, L), ROWS, 1), jax.random.fold_in(key_list[8], 3), 0, ROWS - 1).astype(jnp.int32)
    return {"pooled": pooled, "cotangent": cotangent, "projection": projection, "w_up": w_up, "w_down": w_down, "w_compress": w_compress, "ln_gain": ln_gain, "feature_map": feature_map, "bag_row_index": bag_row_index}


def product(form, left, right):
    return jnp.einsum(form, left.astype(jnp.float32), right.astype(jnp.float32))

def row_norm(values, axis_sel):
    centered_values = values - lax.optimization_barrier(jnp.mean(values, axis=axis_sel, keepdims=True))
    inverse = lax.rsqrt(lax.optimization_barrier(jnp.mean(centered_values * centered_values, axis=axis_sel, keepdims=True)) + 1e-05)
    return (centered_values * inverse, inverse)

def norm_back(grad_in, normed, inverse, axis_sel):
    first = lax.optimization_barrier(jnp.mean(grad_in, axis=axis_sel, keepdims=True))
    second = lax.optimization_barrier(jnp.mean(grad_in * normed, axis=axis_sel, keepdims=True))
    return inverse * (grad_in - first - normed * second)

def forward_backward(pooled, cotangent, projection, w_up, w_down, w_compress, ln_gain):
    batch, width_n, width_d = pooled.shape
    rank = projection.shape[1]
    fm_rows = width_n - w_compress.shape[0]
    proj_part = product('bnd,nk->bdk', pooled, projection).astype(jnp.bfloat16)
    inter = product('bnd,bdk->bnk', pooled, proj_part).reshape(batch, width_n * rank)
    normed_fm, inverse_fm = row_norm(inter, 1)
    normalized_feature_map_batch = normed_fm.astype(jnp.bfloat16)
    preact = product('bi,ih->bh', normalized_feature_map_batch, w_up)
    hidden = jax.nn.silu(preact).astype(jnp.bfloat16)
    fm_out = product('bh,hj->bj', hidden, w_down).reshape(batch, fm_rows, width_d)
    lc_out = product('mn,bnd->bmd', w_compress, pooled)
    summed = jnp.concatenate([fm_out, lc_out], axis=1) + pooled.astype(jnp.float32)
    normed_out, inverse_out = row_norm(summed, 2)
    cot_float = cotangent.astype(jnp.float32)
    grad_gain = lax.optimization_barrier(jnp.sum(cot_float * normed_out, axis=(0, 1)))
    dsum = norm_back(cot_float * ln_gain.astype(jnp.float32), normed_out, inverse_out, 2)
    dfm = dsum[:, :fm_rows].reshape(batch, fm_rows * width_d).astype(jnp.bfloat16)
    dlc = dsum[:, fm_rows:].astype(jnp.bfloat16)
    hidden_gradient = product('bj,hj->bh', dfm, w_down)
    sigmoid_pre = jax.nn.sigmoid(preact)
    dpre = (hidden_gradient * sigmoid_pre * (1.0 + preact * (1.0 - sigmoid_pre))).astype(jnp.bfloat16)
    dnormed = product('bh,ih->bi', dpre, w_up)
    dinter = norm_back(dnormed, normed_fm, inverse_fm, 1).reshape(batch, width_n, rank).astype(jnp.bfloat16)
    dproj = product('bnd,bnk->bdk', pooled, dinter).astype(jnp.bfloat16)
    dpooled = dsum + product('mn,bmd->bnd', w_compress, dlc)
    dpooled = dpooled + product('bnk,bdk->bnd', dinter, proj_part) + product('nk,bdk->bnd', projection, dproj)
    grad_projection = product('bnd,bdk->nk', pooled, dproj)
    compress_weight_gradient = product('bmd,bnd->mn', dlc, pooled)
    return (dpooled.astype(jnp.bfloat16), (normalized_feature_map_batch, dpre, hidden, dfm), (grad_projection, compress_weight_gradient, grad_gain))

def reference(pooled, cotangent, projection, w_up, w_down, w_compress, ln_gain, feature_map, bag_row_index):
    block_size = math.gcd(SAMPLES, 1024)
    nblocks = SAMPLES // block_size

    def one_block(running, inputs):
        pooled_part, cot_part = inputs
        dpooled, (normed_b, dpre, hidden, dfm), (grad_p, grad_c, grad_g) = forward_backward(pooled_part, cot_part, projection, w_up, w_down, w_compress, ln_gain)
        grad_u = product('bi,bh->ih', normed_b, dpre)
        grad_d = product('bh,bj->hj', hidden, dfm)
        updated = (running[0] + grad_u, running[1] + grad_d, running[2] + grad_p, running[3] + grad_c, running[4] + grad_g)
        return (updated, dpooled)
    start_sums = (jnp.zeros((NF * K, H), jnp.float32), jnp.zeros((H, NF_F * E), jnp.float32), jnp.zeros((NF, K), jnp.float32), jnp.zeros((NF_L, NF), jnp.float32), jnp.zeros((E,), jnp.float32))
    totals, dpooled = lax.scan(one_block, start_sums, (pooled.reshape(nblocks, block_size, NF, E), cotangent.reshape(nblocks, block_size, NF, E)))
    dpooled = dpooled.reshape(SAMPLES, NF, E)

    def one_slot(slot_index):
        feature = feature_map[slot_index]
        values = jnp.take(dpooled, feature, axis=1).astype(jnp.float32)
        members = jnp.take(bag_row_index, feature, axis=1).astype(jnp.int32)
        row_total = jnp.zeros((ROWS, E), jnp.float32)
        for position in range(L):
            row_total = row_total + jax.ops.segment_sum(values, members[:, position], num_segments=ROWS)
        return row_total
    table_grad = lax.map(one_slot, jnp.arange(NF, dtype=jnp.int32))
    grad_scale = float(SAMPLES) ** (-0.5)
    return (table_grad, totals[0] * grad_scale, totals[1] * grad_scale, totals[2] * grad_scale, totals[3] * grad_scale, totals[4] * grad_scale)
```

```python
import functools

import jax
import jax.numpy as jnp
from jax import lax
from jax.experimental import pallas as pl
from jax.experimental.pallas import tpu as pltpu
from jax.sharding import Mesh
from jax.sharding import PartitionSpec as P

BF, F32 = jnp.bfloat16, jnp.float32

def dot_nn(a, b):
    return lax.dot_general(a, b, (((1,), (0,)), ((), ())), preferred_element_type=F32)
def dot_nt(a, b):
    return lax.dot_general(a, b, (((1,), (1,)), ((), ())), preferred_element_type=F32)
def dot_tn(a, b):
    return lax.dot_general(a, b, (((0,), (0,)), ((), ())), preferred_element_type=F32)

def out_norm(summed, cot, gain):
    centered = summed - jnp.mean(summed, axis=-1, keepdims=True)
    inverse = lax.rsqrt(jnp.mean(centered * centered, axis=-1, keepdims=True) + 1e-5)
    normed = centered * inverse
    cn = cot * normed
    dnorm = cot * gain
    first = jnp.mean(dnorm, axis=-1, keepdims=True)
    second = jnp.mean(cn * gain, axis=-1, keepdims=True)
    return inverse * (dnorm - first - normed * second), cn

def fold8(v):
    return jnp.sum(v.reshape(v.shape[0] // 8, 8, 128), axis=0)

def fb_kernel(scale, b, fm_ref, pooled_ref, cot_ref, projt_ref, wup_ref, wdown_ref, wc_ref, gain_ref,
              bags_ref, w_ref,
              pf, cf, ds, it, gus, gsmall_ref, ggain_ref, nb_s, dpre_s, hid_s, dfm_s):
    step = pl.program_id(0)
    nsteps = pl.num_programs(0)
    rows = pl.ds(pl.multiple_of(step * b, b), b)
    x = pooled_ref[...]
    pf[...] = x.astype(F32).reshape(b * 64, 128)
    cf[...] = cot_ref[...].astype(F32).reshape(b * 64, 128)
    gain = gain_ref[...]
    projt = projt_ref[...]
    wc = wc_ref[...]
    xcat = jnp.concatenate([x[s] for s in range(b)], axis=1)
    head = dot_nn(jnp.concatenate([projt, wc], axis=0), xcat)
    pts, lcs = [], []
    for s in range(b):
        pts.append(head[0:16, s * 128:(s + 1) * 128].astype(BF))
        lcs.append(head[16:48, s * 128:(s + 1) * 128])
        it[s * 16:(s + 1) * 16, 0:64] = dot_nt(pts[s], x[s])
    inter = jnp.concatenate([it[pl.ds(k, b, stride=16), :][:, 0:64] for k in range(16)], axis=1)
    cen = inter - jnp.mean(inter, axis=1, keepdims=True)
    inv_fm = lax.rsqrt(jnp.mean(cen * cen, axis=1, keepdims=True) + 1e-5)
    normed = cen * inv_fm
    nb = normed.astype(BF)
    nb_s[rows, :] = nb
    preact = dot_nn(nb, wup_ref[...])
    sig = jax.nn.sigmoid(preact)
    hidden = (preact * sig).astype(BF)
    hid_s[rows, :] = hidden
    fm_out = dot_nn(hidden, wdown_ref[...])
    gg = jnp.zeros((8, 128), F32)
    dfms = []
    for m in range(32):
        p_m = pf[pl.ds(m, b, stride=64), :]
        c_m = cf[pl.ds(m, b, stride=64), :]
        dsum, cn = out_norm(fm_out[:, m * 128:(m + 1) * 128] + p_m, c_m, gain)
        gg += fold8(cn)
        ds[pl.ds(m, b, stride=64), :] = dsum
        dfms.append(dsum.astype(BF))
    dlcs = []
    for s in range(b):
        dsum, cn = out_norm(lcs[s] + pf[s * 64 + 32:(s + 1) * 64, :], cf[s * 64 + 32:(s + 1) * 64, :], gain)
        gg += fold8(cn)
        ds[s * 64 + 32:(s + 1) * 64, :] = dsum
        dlcs.append(dsum.astype(BF))
    dfm = jnp.concatenate(dfms, axis=1)
    dfm_s[rows, :] = dfm
    hg = dot_nt(dfm, wdown_ref[...])
    dpre = (hg * sig * (1.0 + preact * (1.0 - sig))).astype(BF)
    dpre_s[rows, :] = dpre
    dnormed = dot_nt(dpre, wup_ref[...])
    first = jnp.mean(dnormed, axis=1, keepdims=True)
    second = jnp.mean(dnormed * normed, axis=1, keepdims=True)
    dinter = (inv_fm * (dnormed - first - normed * second)).astype(BF).astype(F32)
    for k in range(16):
        it[pl.ds(k, b, stride=16), 0:64] = dinter[:, k * 64:(k + 1) * 64]
    tails = []
    for s in range(b):
        dit = it[s * 16:(s + 1) * 16, 0:64].astype(BF)
        dprojt = dot_nn(dit, x[s]).astype(BF)
        tails.append(jnp.concatenate([dlcs[s], dprojt], axis=0))
        left = jnp.concatenate([wc, projt, dit], axis=0)
        right = jnp.concatenate([tails[s], pts[s]], axis=0)
        ds[s * 64:(s + 1) * 64, :] += dot_tn(left, right)
    gsm = dot_nt(jnp.concatenate(tails, axis=1), xcat)
    for j in range(64):
        bags_ref[j, :, :] = ds[pl.ds(fm_ref[j], b, stride=64), :].astype(BF)

    @pl.when(step == 0)
    def _():
        gsmall_ref[...] = gsm
        ggain_ref[...] = gg

    @pl.when(step > 0)
    def _():
        gsmall_ref[...] += gsm
        ggain_ref[...] += gg

    @pl.when(step == nsteps - 1)
    def _():
        for k in range(16):
            part = dot_tn(nb_s[:, k * 64:(k + 1) * 64], dpre_s[...]) * scale
            for q in range(4):
                gus[pl.ds(q * 1024 + k, 64, stride=16), :] = part[:, q * 128:(q + 1) * 128]
        tail = jnp.concatenate([
            jnp.concatenate([gsmall_ref[...], jnp.zeros((48, 64), F32)], axis=1),
            jnp.broadcast_to(jnp.sum(ggain_ref[...], axis=0, keepdims=True), (8, 128)),
            jnp.zeros((8, 128), F32)], axis=0) * scale
        tail = jnp.concatenate([tail[q * 16:(q + 1) * 16, :] for q in range(4)], axis=1).astype(BF)
        for g in range(16):
            for q in range(4):
                w_ref[g, 0:64, q * 128:(q + 1) * 128] = gus[pl.ds(q * 1024 + g * 64, 64), :].astype(BF)
            w_ref[g, 320:336, :] = tail
        for q in range(8):
            part = (dot_tn(hid_s[...], dfm_s[:, q * 512:(q + 1) * 512]) * scale).astype(BF)
            for g in range(16):
                w_ref[g, 64 + q * 32:96 + q * 32, :] = part[g * 32:(g + 1) * 32, :]


def interaction(pooled, cotangent, projection, w_up, w_down, w_compress, ln_gain, feature_map, scale, b=32):
    batch = pooled.shape[0]
    wup = w_up.reshape(64, 16, 512).transpose(1, 0, 2).reshape(1024, 512)
    full = lambda *sh: pl.BlockSpec(sh, lambda i: (0,) * len(sh))
    return pl.pallas_call(
        functools.partial(fb_kernel, scale, b),
        grid=(batch // b,),
        in_specs=[pl.BlockSpec(memory_space=pltpu.SMEM),
                  pl.BlockSpec((b, 64, 128), lambda i: (i, 0, 0)),
                  pl.BlockSpec((b, 64, 128), lambda i: (i, 0, 0)),
                  full(16, 64), full(1024, 512), full(512, 4096), full(32, 64), full(1, 128)],
        out_specs=[pl.BlockSpec((64, b, 128), lambda i: (0, i, 0)),
                   full(16, 336, 512)],
        out_shape=[jax.ShapeDtypeStruct((64, batch, 128), BF),
                   jax.ShapeDtypeStruct((16, 336, 512), BF)],
        scratch_shapes=[pltpu.VMEM((b * 64, 128), F32), pltpu.VMEM((b * 64, 128), F32), pltpu.VMEM((b * 64, 128), F32),
                        pltpu.VMEM((b * 16, 128), F32), pltpu.VMEM((4096, 128), F32),
                        pltpu.VMEM((48, 64), F32), pltpu.VMEM((8, 128), F32),
                        pltpu.VMEM((batch, 1024), BF), pltpu.VMEM((batch, 512), BF),
                        pltpu.VMEM((batch, 512), BF), pltpu.VMEM((batch, 4096), BF)],
        compiler_params=pltpu.CompilerParams(vmem_limit_bytes=56 << 20),
        name="interaction",
    )(feature_map, pooled, cotangent, projection.T, wup, w_down, w_compress, ln_gain.reshape(1, 128))

def table_kernel(mode, src_blk, ids_ref, bags_ref, out_ref, acc):
    step = pl.program_id(1)
    LO, HI = 4, 1024
    ids = ids_ref[:, 0].reshape(src_blk * 2, 128)
    lo = lax.shift_right_logical(ids, 10)
    hi = jnp.bitwise_and(ids, HI - 1)
    cols = jnp.transpose(lo.astype(jnp.float32), (1, 0))
    a_parts, b_parts = [], []
    if mode == "i16":
        iota = lax.broadcasted_iota(jnp.int16, (HI, 128), 0)
        hi16 = hi.astype(jnp.int16)
    else:
        iota = lax.broadcasted_iota(jnp.int32, (HI, 128), 0)
    for i in range(src_blk):
        v = bags_ref[i, 0]
        for t in range(2):
            r = 2 * i + t
            if mode == "i16":
                a = jnp.where(iota == hi16[r:r + 1, :], jnp.bfloat16(1), jnp.bfloat16(0))
            else:
                a = (iota == hi[r:r + 1, :]).astype(jnp.bfloat16)
            a_parts.append(a)
            c = jnp.broadcast_to(cols[:, r:r + 1], (128, 128)).astype(jnp.bfloat16)
            b_parts.append(jnp.concatenate(
                [jnp.where(c == jnp.bfloat16(q), v, jnp.bfloat16(0)) for q in range(LO)], axis=1))
    a = jnp.concatenate(a_parts, axis=1)
    b = jnp.concatenate(b_parts, axis=0)
    part = jnp.dot(a, b, preferred_element_type=jnp.float32)
    @pl.when(step == 0)
    def _():
        acc[...] = part
    @pl.when(step > 0)
    def _():
        acc[...] += part
    @pl.when(step == pl.num_programs(1) - 1)
    def _():
        for q in range(LO):
            out_ref[0, q * HI:(q + 1) * HI, :] = acc[:, q * 128:(q + 1) * 128].astype(out_ref.dtype)

def table_call(ids, bags, mode="i16", src_blk=8, dt=jnp.bfloat16):
    n = bags.shape[0]
    return pl.pallas_call(
        functools.partial(table_kernel, mode, src_blk),
        grid=(2, n // src_blk),
        in_specs=[pl.BlockSpec((src_blk, 1, 2, 128), lambda j, i: (i, j, 0, 0)),
                  pl.BlockSpec((src_blk, 1, 128, 128), lambda j, i: (i, j, 0, 0))],
        out_specs=pl.BlockSpec((1, 4096, 128), lambda j, i: (j, 0, 0)),
        out_shape=jax.ShapeDtypeStruct((2, 4096, 128), dt),
        scratch_shapes=[pltpu.VMEM((1024, 512), jnp.float32)],
        compiler_params=pltpu.CompilerParams(vmem_limit_bytes=48 << 20),
        name="table_" + mode + str(src_blk),
    )(ids, bags)

AXES = ("y", "zh", "x", "zl", "c")
HST = ("y", "zh", "x")
LOCAL = ("zl", "c")
SIZES = (4, 2, 4, 4, 2)


def weight_moves():
    moves = []
    for d in range(256):
        y, zh, x, zl, c = (d // 64, d // 32 % 2, d // 8 % 4, d // 2 % 4, d % 2)
        moves.append((d, ((c * 2 + zh) * 4 + zl) * 16 + y * 4 + x))
    return moves


def shards(pooled, cotangent, projection, w_up, w_down, w_compress, ln_gain, feature_map, bag_row_index):
    batch = pooled.shape[0]
    scale = float(batch * 256) ** (-0.5)
    ids = jnp.take(jnp.transpose(bag_row_index, (1, 2, 0)), feature_map, axis=0)
    ids = lax.all_to_all(ids, ("y", "c", "x"), 0, 0, tiled=True).reshape(32, 2, 2, batch)
    bags, weights = interaction(
        pooled, cotangent, projection, w_up, w_down, w_compress, ln_gain, feature_map, scale)
    halves = lax.all_to_all(weights.reshape(2, 8, 336, 512), "c", 0, 0, tiled=True)
    weights = (halves[0].astype(F32) + halves[1].astype(F32)).astype(BF)
    weights = lax.psum_scatter(weights, ("zh", "zl"), scatter_dimension=0, tiled=True)[0]
    bags = lax.all_to_all(bags, ("y", "c", "x"), 0, 0, tiled=True).reshape(32, 2, batch, 128)
    part = table_call(ids, bags)
    part = lax.psum_scatter(part, ("zl", "zh"), scatter_dimension=1, tiled=True)
    table_grad = lax.ppermute(part, ("zh", "c"), [(0, 0), (1, 2), (2, 1), (3, 3)]).astype(F32)
    pieces = jnp.concatenate(
        [weights[0:64].reshape(16, 4, 512),
         weights[64:320].reshape(8, 16, 2, 512).transpose(1, 0, 2, 3).reshape(16, 16, 512),
         jnp.broadcast_to(weights[320:336], (16, 16, 512))], axis=1)
    pieces = lax.all_to_all(pieces, ("y", "x"), 0, 0, tiled=True)
    total = jnp.sum(pieces.astype(F32), axis=0)
    tail = total[20:36].reshape(16, 4, 128).transpose(1, 0, 2).reshape(64, 128)
    own = lax.ppermute(total[0:20], AXES, weight_moves())
    gd = own[4:20].reshape(8, 2, 512).transpose(1, 0, 2).reshape(2, 4096)
    return (table_grad, own[0:4], gd, tail[32:48, :64].T, tail[:32, :64], tail[48])


def solution(mesh):
    inner = Mesh(mesh.devices.reshape(SIZES), AXES)
    split = P(AXES, None, None)
    return jax.shard_map(
        shards,
        mesh=inner,
        in_specs=(split, split, P(), P(), P(), P(), P(), P(), split),
        out_specs=(P(HST, LOCAL, None), P(AXES, None), P(AXES, None), P(), P(), P()),
        check_vma=False,
    )
```

```python
import functools

import jax
import jax.numpy as jnp
from jax import lax
from jax.experimental import pallas as pl
from jax.experimental.pallas import tpu as pltpu
from jax.sharding import Mesh
from jax.sharding import PartitionSpec as P

BF, F32 = jnp.bfloat16, jnp.float32


def dot_nn(a, b):
    return lax.dot_general(a, b, (((1,), (0,)), ((), ())), preferred_element_type=F32)


def dot_nt(a, b):
    return lax.dot_general(a, b, (((1,), (1,)), ((), ())), preferred_element_type=F32)


def dot_tn(a, b):
    return lax.dot_general(a, b, (((0,), (0,)), ((), ())), preferred_element_type=F32)


def out_norm(summed, cot, gain):
    centered = summed - jnp.mean(summed, axis=-1, keepdims=True)
    inverse = lax.rsqrt(jnp.mean(centered * centered, axis=-1, keepdims=True) + 1e-5)
    normed = centered * inverse
    cot_normed = cot * normed
    dnorm = cot * gain
    first = jnp.mean(dnorm, axis=-1, keepdims=True)
    second = jnp.mean(cot_normed * gain, axis=-1, keepdims=True)
    return inverse * (dnorm - first - normed * second), cot_normed


def fold8(v):
    return jnp.sum(v.reshape(v.shape[0] // 8, 8, 128), axis=0)


def layer_kernel(scale, b, fm_ref, pooled_ref, cot_ref, proj_ref, wup_ref, wdown_ref, wc_ref, gain_ref,
                 bags_ref, acts_ref, tail_ref, inv_ref, ds1, ds2, wups, wupr):
    for j in range(64):
        inv_ref[fm_ref[j]] = j
    for q in range(4):
        wups[...] = wup_ref[:, q * 128:(q + 1) * 128].astype(F32)
        for k in range(16):
            wupr[k * 64:(k + 1) * 64, q * 128:(q + 1) * 128] = wups[pl.ds(k, 64, stride=16), :].astype(BF)
    x = pooled_ref[...]
    gain = gain_ref[...]
    proj = proj_ref[...]
    wc = wc_ref[...]
    projt = jnp.transpose(proj.astype(F32)).astype(BF)
    consts = jnp.concatenate([jnp.transpose(wc.astype(F32)).astype(BF), proj], axis=1)
    xcat = jnp.concatenate([x[s] for s in range(b)], axis=1)
    head = dot_nn(jnp.concatenate([projt, wc], axis=0), xcat)
    pts = [head[0:16, s * 128:(s + 1) * 128].astype(BF) for s in range(b)]
    inter = jnp.stack([dot_nt(pts[s], x[s]) for s in range(b)], axis=0)
    inter = jnp.swapaxes(inter, 0, 1)
    inter = jnp.concatenate([inter[k] for k in range(16)], axis=1)
    cen = inter - jnp.mean(inter, axis=1, keepdims=True)
    inv_fm = lax.rsqrt(jnp.mean(cen * cen, axis=1, keepdims=True) + 1e-5)
    normed = cen * inv_fm
    nb = normed.astype(BF)
    preact = dot_nn(nb, wupr[...])
    sig = jax.nn.sigmoid(preact)
    hidden = (preact * sig).astype(BF)
    fm_out = dot_nn(hidden, wdown_ref[...])
    gg = jnp.zeros((8, 128), F32)
    dfms = []
    for m in range(32):
        if m % 16 == 0:
            xf = jnp.swapaxes(pooled_ref[:, m:m + 16, :], 0, 1)
            cf = jnp.swapaxes(cot_ref[:, m:m + 16, :], 0, 1)
        dsum, cot_normed = out_norm(
            fm_out[:, m * 128:(m + 1) * 128] + xf[m % 16].astype(F32), cf[m % 16].astype(F32), gain)
        gg += fold8(cot_normed)
        ds1[m] = dsum
        dfms.append(dsum.astype(BF))
    dlcs = []
    for s in range(b):
        dsum, cot_normed = out_norm(
            head[16:48, s * 128:(s + 1) * 128] + x[s, 32:64].astype(F32), cot_ref[s, 32:64, :].astype(F32), gain)
        gg += fold8(cot_normed)
        ds2[s] = dsum
        dlcs.append(dsum.astype(BF))
    dfm = jnp.concatenate(dfms, axis=1)
    hg = dot_nt(dfm, wdown_ref[...])
    dpre = (hg * sig * (1.0 + preact * (1.0 - sig))).astype(BF)
    for h in range(2):
        acts_ref[h, :, 0:512] = nb[:, h * 512:(h + 1) * 512]
        acts_ref[h, :, 512:1024] = dpre
        acts_ref[h, :, 1024:1280] = hidden[:, h * 256:(h + 1) * 256]
        acts_ref[h, :, 1280:5376] = dfm
    dnormed = dot_nt(dpre, wupr[...])
    first = jnp.mean(dnormed, axis=1, keepdims=True)
    second = jnp.mean(dnormed * normed, axis=1, keepdims=True)
    dinter = (inv_fm * (dnormed - first - normed * second)).astype(BF).astype(F32)
    dinter = jnp.swapaxes(jnp.stack([dinter[:, k * 64:(k + 1) * 64] for k in range(16)], axis=0), 0, 1)
    zero = jnp.zeros((16, 128), BF)
    tails = []
    for g in range(b // 16):
        outs = []
        for half in range(2):
            group = [g * 16 + half * 8 + i for i in range(8)]
            for s in group:
                dproj = dot_nn(dinter[s].astype(BF), x[s]).astype(BF)
                tails.append(jnp.concatenate([dlcs[s], dproj], axis=0))
            block = dinter[group[0]:group[0] + 8].reshape(128, 64)
            left = jnp.concatenate([jnp.transpose(block).astype(BF), consts], axis=1)
            right = jnp.concatenate(
                [jnp.concatenate([pts[s] if i == r else zero for i, s in enumerate(group)], axis=1) for r in range(8)]
                + [jnp.concatenate([tails[s] for s in group], axis=1)], axis=0)
            res = dot_nn(left, right)
            outs += [res[:, i * 128:(i + 1) * 128] for i in range(8)]
        for n in range(8):
            rows = [v[n * 8:(n + 1) * 8] for v in outs]
            if n >= 4:
                rows = [v + ds2[g * 16 + i, (n - 4) * 8:(n - 3) * 8, :] for i, v in enumerate(rows)]
            turned = jnp.swapaxes(jnp.stack(rows, axis=0), 0, 1)
            for i in range(8):
                v = turned[i]
                if n < 4:
                    v = v + ds1[n * 8 + i, g * 16:(g + 1) * 16, :]
                bags_ref[inv_ref[n * 8 + i], g * 16:(g + 1) * 16, :] = v.astype(BF)
    gsm = dot_nt(jnp.concatenate(tails, axis=1), xcat)
    tail_ref[...] = jnp.concatenate([
        jnp.concatenate([gsm, jnp.zeros((48, 64), F32)], axis=1),
        jnp.broadcast_to(jnp.sum(gg, axis=0, keepdims=True), (16, 128))], axis=0) * scale


def layer_call(part, batch, feature_map, pooled, cotangent, projection, w_up, w_down, w_compress, gain, scale):
    full = lambda *sh: pl.BlockSpec(sh, lambda i: (0,) * len(sh))
    half = lambda: pl.BlockSpec((batch, 64, 128), lambda i: (part, 0, 0))
    return pl.pallas_call(
        functools.partial(layer_kernel, scale, batch),
        grid=(1,),
        in_specs=[pl.BlockSpec(memory_space=pltpu.SMEM), half(), half(),
                  full(64, 16), full(1024, 512), full(512, 4096), full(32, 64), full(1, 128)],
        out_specs=[full(64, batch, 128), full(2, batch, 5376), full(64, 128)],
        out_shape=[jax.ShapeDtypeStruct((64, batch, 128), BF),
                   jax.ShapeDtypeStruct((2, batch, 5376), BF),
                   jax.ShapeDtypeStruct((64, 128), F32)],
        scratch_shapes=[pltpu.SMEM((64,), jnp.int32),
                        pltpu.VMEM((32, batch, 128), F32), pltpu.VMEM((batch, 32, 128), F32),
                        pltpu.VMEM((1024, 128), F32), pltpu.VMEM((1024, 512), BF)],
        compiler_params=pltpu.CompilerParams(vmem_limit_bytes=50 << 20),
        cost_estimate=pl.CostEstimate(flops=15 * 10**9, bytes_accessed=10 << 20, transcendentals=0),
        name="layer",
    )(feature_map, pooled, cotangent, projection, w_up, w_down, w_compress, gain)


def weight_kernel(scale, acts0_ref, acts1_ref, tail0_ref, tail1_ref, w_ref, gus):
    acts = jnp.concatenate([acts0_ref[0], acts0_ref[1], acts1_ref[0], acts1_ref[1]], axis=0)
    tail = tail0_ref[...] + tail1_ref[...]
    tail = jnp.concatenate([tail[q * 16:(q + 1) * 16, :] for q in range(4)], axis=1).astype(BF)
    up = dot_tn(acts[:, 0:512], acts[:, 512:1024]) * scale
    for q in range(4):
        for k in range(8):
            gus[pl.ds(k, 64, stride=8), :] = up[k * 64:(k + 1) * 64, q * 128:(q + 1) * 128]
        for z in range(16):
            w_ref[z, 0:32, q * 128:(q + 1) * 128] = gus[z * 32:(z + 1) * 32, :].astype(BF)
    hid = acts[:, 1024:1280]
    for q in range(8):
        down = (dot_tn(hid, acts[:, 1280 + q * 512:1792 + q * 512]) * scale).astype(BF)
        for z in range(16):
            w_ref[z, 32 + q * 16:48 + q * 16, :] = down[z * 16:(z + 1) * 16, :]
    for z in range(16):
        w_ref[z, 160:176, :] = tail


def weight_call(acts0, acts1, tail0, tail1, scale):
    return pl.pallas_call(
        functools.partial(weight_kernel, scale),
        out_shape=jax.ShapeDtypeStruct((16, 176, 512), BF),
        scratch_shapes=[pltpu.VMEM((512, 128), F32)],
        compiler_params=pltpu.CompilerParams(vmem_limit_bytes=40 << 20),
        cost_estimate=pl.CostEstimate(flops=5 * 10**9, bytes_accessed=6 << 20, transcendentals=0),
        name="weight_grads",
    )(acts0, acts1, tail0, tail1)


def table_kernel(pairs, last, *refs):
    if last:
        ids_ref, bags_ref, start_ref, out_ref, acc = refs
    else:
        ids_ref, bags_ref, acc = refs
        acc = acc.at[0]
    step = pl.program_id(1)
    ids = ids_ref[:, 0].reshape(pairs * 2, 128)
    low = jnp.transpose(lax.shift_right_logical(ids, 10).astype(F32), (1, 0))
    high = jnp.bitwise_and(ids, 1023).astype(jnp.int16)
    iota = lax.broadcasted_iota(jnp.int16, (1024, 128), 0)
    left, right = [], []
    for i in range(pairs):
        values = bags_ref[i, :, 0].reshape(128, 128)
        for t in range(2):
            r = 2 * i + t
            left.append(jnp.where(iota == high[r:r + 1, :], jnp.bfloat16(1), jnp.bfloat16(0)))
            column = jnp.broadcast_to(low[:, r:r + 1], (128, 128)).astype(BF)
            right.append(jnp.concatenate(
                [jnp.where(column == jnp.bfloat16(q), values, jnp.bfloat16(0)) for q in range(4)], axis=1))
    part = jnp.dot(jnp.concatenate(left, axis=1), jnp.concatenate(right, axis=0), preferred_element_type=F32)

    @pl.when(step == 0)
    def _():
        acc[...] = start_ref[0] + part if last else part

    @pl.when(step > 0)
    def _():
        acc[...] += part

    if last:
        @pl.when(step == pl.num_programs(1) - 1)
        def _():
            for q in range(4):
                for h in range(2):
                    out_ref[h * 4 + q, 0] = acc[h * 512:(h + 1) * 512, q * 128:(q + 1) * 128].astype(BF)


def table_call(ids, bags, start=None, pairs=8):
    last = start is not None
    sums = pl.BlockSpec((1, 1024, 512), lambda j, i: (j, 0, 0))
    return pl.pallas_call(
        functools.partial(table_kernel, pairs, last),
        grid=(2, ids.shape[0] // pairs),
        in_specs=[pl.BlockSpec((pairs, 1, 2, 128), lambda j, i: (i, j, 0, 0)),
                  pl.BlockSpec((pairs, 2, 1, 64, 128), lambda j, i: (i, 0, j, 0, 0))] + ([sums] if last else []),
        out_specs=pl.BlockSpec((8, 1, 512, 128), lambda j, i: (0, j, 0, 0)) if last else sums,
        out_shape=jax.ShapeDtypeStruct((8, 2, 512, 128), BF) if last else jax.ShapeDtypeStruct((2, 1024, 512), F32),
        scratch_shapes=[pltpu.VMEM((1024, 512), F32)] if last else [],
        compiler_params=pltpu.CompilerParams(vmem_limit_bytes=48 << 20),
        cost_estimate=pl.CostEstimate(flops=9 * 10**9, bytes_accessed=5 << 20, transcendentals=0),
        name="table_last" if last else "table_first",
    )(*([ids, bags] + ([start] if last else [])))


AXES = ("y", "zh", "x", "zl", "c")
HST = ("y", "zh", "x")
LOCAL = ("zl", "c")
SIZES = (4, 2, 4, 4, 2)
PLANE = ("y", "c", "x")


def weight_moves():
    up, down = [], []
    for d in range(256):
        y, zh, x, zl, c = (d // 64, d // 32 % 2, d // 8 % 4, d // 2 % 4, d % 2)
        unit = (y * 4 + x) * 8 + zh * 4 + zl
        up.append((d, (unit // 2) * 4 + 2 * c + unit % 2))
        down.append((d, c * 128 + unit))
    return up, down


def shards(pooled, cotangent, projection, w_up, w_down, w_compress, ln_gain, feature_map, bag_row_index):
    batch = pooled.shape[0] // 2
    scale = float(batch * 512) ** (-0.5)
    ids = jnp.take(jnp.transpose(bag_row_index, (1, 2, 0)), feature_map, axis=0)
    ids = lax.all_to_all(ids, PLANE, 0, 0, tiled=True).reshape(16, 2, 2, 2, 2, batch)
    ids = jnp.transpose(ids, (4, 0, 2, 3, 1, 5)).reshape(2, 16, 2, 2, 128)
    bags, acts, tails = [], [], []
    for part in range(2):
        bag, act, tail = layer_call(
            part, batch, feature_map, pooled, cotangent, projection, w_up, w_down, w_compress,
            ln_gain.reshape(1, 128), scale)
        bags.append(lax.all_to_all(bag, PLANE, 0, 0, tiled=True).reshape(16, 2, 2, batch, 128))
        acts.append(lax.all_to_all(act, "c", 0, 0, tiled=True))
        tails.append(tail)
    weights = weight_call(acts[0], acts[1], tails[0], tails[1], scale)
    weights = lax.all_to_all(weights, ("y", "x"), 0, 0, tiled=True)
    sums = table_call(ids[0], bags[0])
    rows = table_call(ids[1], bags[1], sums)
    rows = lax.psum_scatter(rows, ("zh", "zl"), scatter_dimension=0, tiled=True)[0]
    weights = jnp.sum(weights.astype(F32), axis=0).astype(BF)
    pieces = jnp.concatenate(
        [weights[0:32].reshape(8, 4, 512),
         weights[32:160].reshape(8, 8, 2, 512).transpose(1, 0, 2, 3).reshape(8, 16, 512),
         jnp.broadcast_to(weights[160:176], (8, 16, 512))], axis=1)
    pieces = lax.all_to_all(pieces, ("zh", "zl"), 0, 0, tiled=True)
    total = jnp.sum(pieces.astype(F32), axis=0)
    up_moves, down_moves = weight_moves()
    gu = lax.ppermute(total[0:4], AXES, up_moves)
    gd = lax.ppermute(total[4:20], AXES, down_moves).reshape(8, 2, 512).transpose(1, 0, 2).reshape(2, 4096)
    tail = total[20:36].reshape(16, 4, 128).transpose(1, 0, 2).reshape(64, 128)
    tail = tail + lax.ppermute(tail, "c", [(0, 1), (1, 0)])
    small = (tail[32:48, :64].T, tail[:32, :64], tail[48])
    rows, gu, gd, small = lax.optimization_barrier((rows, gu, gd, small))
    table_grad = lax.ppermute(rows, ("zh", "c"), [(0, 0), (1, 2), (2, 1), (3, 3)]).astype(F32)
    return (table_grad, gu, gd) + tuple(small)


def solution(mesh):
    inner = Mesh(mesh.devices.reshape(SIZES), AXES)
    split = P(AXES, None, None)
    return jax.shard_map(
        shards,
        mesh=inner,
        in_specs=(split, split, P(), P(), P(), P(), P(), P(), split),
        out_specs=(P(HST, LOCAL, None), P(AXES, None), P(AXES, None), P(), P(), P()),
        check_vma=False,
    )
```

```python
import functools

import jax
import jax.numpy as jnp
from jax import lax
from jax.experimental import pallas as pl
from jax.experimental.pallas import tpu as pltpu
from jax.sharding import Mesh
from jax.sharding import PartitionSpec as P

BF, F32 = jnp.bfloat16, jnp.float32


def dot_nn(a, b):
    return lax.dot_general(a, b, (((1,), (0,)), ((), ())), preferred_element_type=F32)


def dot_nt(a, b):
    return lax.dot_general(a, b, (((1,), (1,)), ((), ())), preferred_element_type=F32)


def dot_tn(a, b):
    return lax.dot_general(a, b, (((0,), (0,)), ((), ())), preferred_element_type=F32)


def out_norm(summed, cot, gain):
    centered = summed - jnp.mean(summed, axis=-1, keepdims=True)
    inverse = lax.rsqrt(jnp.mean(centered * centered, axis=-1, keepdims=True) + 1e-5)
    normed = centered * inverse
    cot_normed = cot * normed
    dnorm = cot * gain
    first = jnp.mean(dnorm, axis=-1, keepdims=True)
    second = jnp.mean(cot_normed * gain, axis=-1, keepdims=True)
    return inverse * (dnorm - first - normed * second), cot_normed


def fold8(v):
    return jnp.sum(v.reshape(v.shape[0] // 8, 8, 128), axis=0)


def layer_kernel(scale, b, fm_ref, core_ref, pooled_ref, cot_ref, proj_ref, wup_ref, wdown_ref, wc_ref, gain_ref,
                 bags_ref, keep_ref, send_ref, tail_ref, inv_ref, ds1, ds2, wups, wupr):
    for j in range(64):
        inv_ref[fm_ref[j]] = j
    for q in range(4):
        wups[...] = wup_ref[:, q * 128:(q + 1) * 128].astype(F32)
        for k in range(16):
            wupr[k * 64:(k + 1) * 64, q * 128:(q + 1) * 128] = wups[pl.ds(k, 64, stride=16), :].astype(BF)
    x = pooled_ref[...]
    gain = gain_ref[...]
    proj = proj_ref[...]
    wc = wc_ref[...]
    projt = jnp.transpose(proj.astype(F32)).astype(BF)
    consts = jnp.concatenate([jnp.transpose(wc.astype(F32)).astype(BF), proj], axis=1)
    xcat = jnp.concatenate([x[s] for s in range(b)], axis=1)
    head = dot_nn(jnp.concatenate([projt, wc], axis=0), xcat)
    pts = [head[0:16, s * 128:(s + 1) * 128].astype(BF) for s in range(b)]
    inter = jnp.stack([dot_nt(pts[s], x[s]) for s in range(b)], axis=0)
    inter = jnp.swapaxes(inter, 0, 1)
    inter = jnp.concatenate([inter[k] for k in range(16)], axis=1)
    cen = inter - jnp.mean(inter, axis=1, keepdims=True)
    inv_fm = lax.rsqrt(jnp.mean(cen * cen, axis=1, keepdims=True) + 1e-5)
    normed = cen * inv_fm
    nb = normed.astype(BF)
    preact = dot_nn(nb, wupr[...])
    sig = jax.nn.sigmoid(preact)
    hidden = (preact * sig).astype(BF)
    fm_out = dot_nn(hidden, wdown_ref[...])
    gg = jnp.zeros((8, 128), F32)
    dfms = []
    for m in range(32):
        if m % 16 == 0:
            xf = jnp.swapaxes(pooled_ref[:, m:m + 16, :], 0, 1)
            cf = jnp.swapaxes(cot_ref[:, m:m + 16, :], 0, 1)
        dsum, cot_normed = out_norm(
            fm_out[:, m * 128:(m + 1) * 128] + xf[m % 16].astype(F32), cf[m % 16].astype(F32), gain)
        gg += fold8(cot_normed)
        ds1[m] = dsum
        dfms.append(dsum.astype(BF))
    dlcs = []
    for s in range(b):
        dsum, cot_normed = out_norm(
            head[16:48, s * 128:(s + 1) * 128] + x[s, 32:64].astype(F32), cot_ref[s, 32:64, :].astype(F32), gain)
        gg += fold8(cot_normed)
        ds2[s] = dsum
        dlcs.append(dsum.astype(BF))
    dfm = jnp.concatenate(dfms, axis=1)
    hg = dot_nt(dfm, wdown_ref[...])
    dpre = (hg * sig * (1.0 + preact * (1.0 - sig))).astype(BF)
    first_core = core_ref[0] == 0
    for ref, flag in ((keep_ref, first_core), (send_ref, jnp.logical_not(first_core))):
        ref[:, 0:512] = jnp.where(flag, nb[:, 0:512], nb[:, 512:1024])
        ref[:, 512:1024] = dpre
        ref[:, 1024:1280] = jnp.where(flag, hidden[:, 0:256], hidden[:, 256:512])
        ref[:, 1280:5376] = dfm
    dnormed = dot_nt(dpre, wupr[...])
    first = jnp.mean(dnormed, axis=1, keepdims=True)
    second = jnp.mean(dnormed * normed, axis=1, keepdims=True)
    dinter = (inv_fm * (dnormed - first - normed * second)).astype(BF).astype(F32)
    dinter = jnp.swapaxes(jnp.stack([dinter[:, k * 64:(k + 1) * 64] for k in range(16)], axis=0), 0, 1)
    zero = jnp.zeros((16, 128), BF)
    tails = []
    for g in range(b // 16):
        outs = []
        for half in range(2):
            group = [g * 16 + half * 8 + i for i in range(8)]
            for s in group:
                dproj = dot_nn(dinter[s].astype(BF), x[s]).astype(BF)
                tails.append(jnp.concatenate([dlcs[s], dproj], axis=0))
            block = dinter[group[0]:group[0] + 8].reshape(128, 64)
            left = jnp.concatenate([jnp.transpose(block).astype(BF), consts], axis=1)
            right = jnp.concatenate(
                [jnp.concatenate([pts[s] if i == r else zero for i, s in enumerate(group)], axis=1) for r in range(8)]
                + [jnp.concatenate([tails[s] for s in group], axis=1)], axis=0)
            res = dot_nn(left, right)
            outs += [res[:, i * 128:(i + 1) * 128] for i in range(8)]
        for n in range(8):
            rows = [v[n * 8:(n + 1) * 8] for v in outs]
            if n >= 4:
                rows = [v + ds2[g * 16 + i, (n - 4) * 8:(n - 3) * 8, :] for i, v in enumerate(rows)]
            turned = jnp.swapaxes(jnp.stack(rows, axis=0), 0, 1)
            for i in range(8):
                v = turned[i]
                if n < 4:
                    v = v + ds1[n * 8 + i, g * 16:(g + 1) * 16, :]
                bags_ref[inv_ref[n * 8 + i], g * 16:(g + 1) * 16, :] = v.astype(BF)
    gsm = dot_nt(jnp.concatenate(tails, axis=1), xcat)
    tail_ref[...] = jnp.concatenate([
        jnp.concatenate([gsm, jnp.zeros((48, 64), F32)], axis=1),
        jnp.broadcast_to(jnp.sum(gg, axis=0, keepdims=True), (16, 128))], axis=0) * scale


def layer_call(part, batch, feature_map, core, pooled, cotangent, projection, w_up, w_down, w_compress, gain, scale):
    full = lambda *sh: pl.BlockSpec(sh, lambda i: (0,) * len(sh))
    half = lambda: pl.BlockSpec((batch, 64, 128), lambda i: (part, 0, 0))
    return pl.pallas_call(
        functools.partial(layer_kernel, scale, batch),
        grid=(1,),
        in_specs=[pl.BlockSpec(memory_space=pltpu.SMEM), pl.BlockSpec(memory_space=pltpu.SMEM), half(), half(),
                  full(64, 16), full(1024, 512), full(512, 4096), full(32, 64), full(1, 128)],
        out_specs=[full(64, batch, 128), full(batch, 5376), full(batch, 5376), full(64, 128)],
        out_shape=[jax.ShapeDtypeStruct((64, batch, 128), BF),
                   jax.ShapeDtypeStruct((batch, 5376), BF),
                   jax.ShapeDtypeStruct((batch, 5376), BF),
                   jax.ShapeDtypeStruct((64, 128), F32)],
        scratch_shapes=[pltpu.SMEM((64,), jnp.int32),
                        pltpu.VMEM((32, batch, 128), F32), pltpu.VMEM((batch, 32, 128), F32),
                        pltpu.VMEM((1024, 128), F32), pltpu.VMEM((1024, 512), BF)],
        compiler_params=pltpu.CompilerParams(vmem_limit_bytes=50 << 20),
        cost_estimate=pl.CostEstimate(flops=15 * 10**9, bytes_accessed=10 << 20, transcendentals=0),
        name="layer",
    )(feature_map, core, pooled, cotangent, projection, w_up, w_down, w_compress, gain)


def weight_kernel(scale, a0_ref, b0_ref, a1_ref, b1_ref, tail0_ref, tail1_ref, w_ref, gus):
    acts = jnp.concatenate([a0_ref[...], b0_ref[...], a1_ref[...], b1_ref[...]], axis=0)
    tail = tail0_ref[...] + tail1_ref[...]
    tail = jnp.concatenate([tail[q * 16:(q + 1) * 16, :] for q in range(4)], axis=1).astype(BF)
    up = dot_tn(acts[:, 0:512], acts[:, 512:1024]) * scale
    for q in range(4):
        for k in range(8):
            gus[pl.ds(k, 64, stride=8), :] = up[k * 64:(k + 1) * 64, q * 128:(q + 1) * 128]
        for z in range(8):
            w_ref[z, 0:64, q * 128:(q + 1) * 128] = gus[z * 64:(z + 1) * 64, :].astype(BF)
    hid = acts[:, 1024:1280]
    for q in range(8):
        down = (dot_tn(hid, acts[:, 1280 + q * 512:1792 + q * 512]) * scale).astype(BF)
        for z in range(8):
            w_ref[z, 64 + q * 32:96 + q * 32, :] = down[z * 32:(z + 1) * 32, :]
    for z in range(8):
        w_ref[z, 320:336, :] = tail


def weight_call(acts, tails, scale):
    return pl.pallas_call(
        functools.partial(weight_kernel, scale),
        out_shape=jax.ShapeDtypeStruct((8, 336, 512), BF),
        scratch_shapes=[pltpu.VMEM((512, 128), F32)],
        compiler_params=pltpu.CompilerParams(vmem_limit_bytes=40 << 20),
        cost_estimate=pl.CostEstimate(flops=3 * 10**9, bytes_accessed=6 << 20, transcendentals=0),
        name="weight_grads",
    )(*acts, *tails)


def table_kernel(pairs, last, *refs):
    if last:
        ids_ref, bags_ref, start_ref, out_ref, acc = refs
    else:
        ids_ref, bags_ref, acc = refs
        acc = acc.at[0]
    step = pl.program_id(1)
    ids = ids_ref[:, 0].reshape(pairs * 2, 128)
    low = jnp.transpose(lax.shift_right_logical(ids, 10).astype(F32), (1, 0))
    high = jnp.bitwise_and(ids, 1023).astype(jnp.int16)
    iota = lax.broadcasted_iota(jnp.int16, (1024, 128), 0)
    left, right = [], []
    for i in range(pairs):
        values = bags_ref[i, :, 0].reshape(128, 128)
        for t in range(2):
            r = 2 * i + t
            left.append(jnp.where(iota == high[r:r + 1, :], jnp.bfloat16(1), jnp.bfloat16(0)))
            column = jnp.broadcast_to(low[:, r:r + 1], (128, 128)).astype(BF)
            right.append(jnp.concatenate(
                [jnp.where(column == jnp.bfloat16(q), values, jnp.bfloat16(0)) for q in range(4)], axis=1))
    part = jnp.dot(jnp.concatenate(left, axis=1), jnp.concatenate(right, axis=0), preferred_element_type=F32)

    @pl.when(step == 0)
    def _():
        acc[...] = start_ref[0] + part if last else part

    @pl.when(step > 0)
    def _():
        acc[...] += part

    if last:
        @pl.when(step == pl.num_programs(1) - 1)
        def _():
            for q in range(4):
                for h in range(2):
                    out_ref[h * 4 + q, 0] = acc[h * 512:(h + 1) * 512, q * 128:(q + 1) * 128].astype(BF)


def table_call(ids, bags, start=None, pairs=8):
    last = start is not None
    sums = pl.BlockSpec((1, 1024, 512), lambda j, i: (j, 0, 0))
    return pl.pallas_call(
        functools.partial(table_kernel, pairs, last),
        grid=(2, ids.shape[0] // pairs),
        in_specs=[pl.BlockSpec((pairs, 1, 2, 128), lambda j, i: (i, j, 0, 0)),
                  pl.BlockSpec((pairs, 2, 1, 64, 128), lambda j, i: (i, 0, j, 0, 0))] + ([sums] if last else []),
        out_specs=pl.BlockSpec((8, 1, 512, 128), lambda j, i: (0, j, 0, 0)) if last else sums,
        out_shape=jax.ShapeDtypeStruct((8, 2, 512, 128), BF) if last else jax.ShapeDtypeStruct((2, 1024, 512), F32),
        scratch_shapes=[pltpu.VMEM((1024, 512), F32)] if last else [],
        compiler_params=pltpu.CompilerParams(vmem_limit_bytes=48 << 20),
        cost_estimate=pl.CostEstimate(flops=9 * 10**9, bytes_accessed=5 << 20, transcendentals=0),
        name="table_last" if last else "table_first",
    )(*([ids, bags] + ([start] if last else [])))


AXES = ("y", "zh", "x", "zl", "c")
HST = ("y", "zh", "x")
LOCAL = ("zl", "c")
SIZES = (4, 2, 4, 4, 2)
PLANE = ("y", "c", "x")


def weight_moves():
    up, down = [], []
    for d in range(256):
        y, zh, x, zl, c = (d // 64, d // 32 % 2, d // 8 % 4, d // 2 % 4, d % 2)
        z, sub = zh * 4 + zl, y * 4 + x
        up.append((d, z * 32 + (sub // 2) * 4 + 2 * c + sub % 2))
        down.append((d, c * 128 + z * 16 + sub))
    return up, down


def shards(pooled, cotangent, projection, w_up, w_down, w_compress, ln_gain, feature_map, bag_row_index):
    batch = pooled.shape[0] // 2
    scale = float(batch * 512) ** (-0.5)
    core = lax.axis_index("c").astype(jnp.int32).reshape(1)
    ids = jnp.take(jnp.transpose(bag_row_index, (1, 2, 0)), feature_map, axis=0)
    ids = lax.all_to_all(ids, PLANE, 0, 0, tiled=True)
    swap = [(0, 1), (1, 0)]

    def layer(part):
        return layer_call(part, batch, feature_map, core, pooled, cotangent, projection, w_up, w_down, w_compress,
                          ln_gain.reshape(1, 128), scale)

    def exchange(bag):
        return lax.all_to_all(bag, PLANE, 0, 0, tiled=True)

    bag0, keep0, send0, tail0 = layer(0)
    bag0, ids = lax.optimization_barrier((bag0, ids))
    ids = jnp.transpose(ids.reshape(16, 2, 2, 2, 2, batch), (4, 0, 2, 3, 1, 5)).reshape(2, 16, 2, 2, 128)
    first = exchange(bag0)
    bag1, keep1, send1, tail1 = layer(1)
    send1, first = lax.optimization_barrier((send1, first))
    acts = (keep0, lax.ppermute(send0, "c", swap), keep1, lax.ppermute(send1, "c", swap))
    weights = weight_call(acts, (tail0, tail1), scale)
    bag1, weights = lax.optimization_barrier((bag1, weights))
    weights = lax.psum_scatter(weights.reshape(8 * 336, 512), ("zh", "zl"), scatter_dimension=0, tiled=True)
    second = exchange(bag1)
    rows = table_call(ids[0], first.reshape(16, 2, 2, batch, 128))
    rows = table_call(ids[1], second.reshape(16, 2, 2, batch, 128), rows)
    weights, _ = lax.optimization_barrier((weights, rows))
    rows = lax.psum_scatter(rows.reshape(8192, 128), ("zh", "zl"), scatter_dimension=0, tiled=True)
    pieces = jnp.concatenate(
        [weights[0:64].reshape(16, 4, 512),
         weights[64:320].reshape(8, 16, 2, 512).transpose(1, 0, 2, 3).reshape(16, 16, 512),
         jnp.broadcast_to(weights[320:336], (16, 16, 512))], axis=1)
    pieces = lax.all_to_all(pieces, ("y", "x"), 0, 0, tiled=True)
    total = jnp.sum(pieces.astype(F32), axis=0)
    up_moves, down_moves = weight_moves()
    gu = lax.ppermute(total[0:4], AXES, up_moves)
    gd = lax.ppermute(total[4:20], AXES, down_moves).reshape(8, 2, 512).transpose(1, 0, 2).reshape(2, 4096)
    tail = total[20:36].reshape(16, 4, 128).transpose(1, 0, 2).reshape(64, 128)
    tail = tail + lax.ppermute(tail, "c", swap)
    small = (tail[32:48, :64].T, tail[:32, :64], tail[48])
    rows, gu, gd, small = lax.optimization_barrier((rows, gu, gd, small))
    table_grad = lax.ppermute(rows, ("zh", "c"), [(0, 0), (1, 2), (2, 1), (3, 3)]).astype(F32)
    return (table_grad.reshape(2, 512, 128), gu, gd) + tuple(small)


def solution(mesh):
    inner = Mesh(mesh.devices.reshape(SIZES), AXES)
    split = P(AXES, None, None)
    return jax.shard_map(
        shards,
        mesh=inner,
        in_specs=(split, split, P(), P(), P(), P(), P(), P(), split),
        out_specs=(P(HST, LOCAL, None), P(AXES, None), P(AXES, None), P(), P(), P()),
        check_vma=False,
    )
```

```python
import functools

import jax
import jax.numpy as jnp
from jax import lax
from jax.experimental import pallas as pl
from jax.experimental.pallas import tpu as pltpu
from jax.sharding import Mesh
from jax.sharding import PartitionSpec as P

BF, F32 = jnp.bfloat16, jnp.float32
VMEM_BYTES = 60 << 20


def dot_nn(a, b):
    return lax.dot_general(a, b, (((1,), (0,)), ((), ())), preferred_element_type=F32)


def dot_nt(a, b):
    return lax.dot_general(a, b, (((1,), (1,)), ((), ())), preferred_element_type=F32)


def dot_tn(a, b):
    return lax.dot_general(a, b, (((0,), (0,)), ((), ())), preferred_element_type=F32)


def out_norm(summed, cot, gain):
    centered = summed - jnp.mean(summed, axis=-1, keepdims=True)
    inverse = lax.rsqrt(jnp.mean(centered * centered, axis=-1, keepdims=True) + 1e-5)
    normed = centered * inverse
    cot_normed = cot * normed
    dnorm = cot * gain
    first = jnp.mean(dnorm, axis=-1, keepdims=True)
    second = jnp.mean(cot_normed * gain, axis=-1, keepdims=True)
    return inverse * (dnorm - first - normed * second), cot_normed


def fold8(v):
    return jnp.sum(v.reshape(v.shape[0] // 8, 8, 128), axis=0)


def layer_kernel(scale, b, part, with_ids, *refs):
    fm_ref, core_ref, pooled_ref = refs[:3]
    ids_ref = refs[3] if with_ids else None
    (cot_hbm, projt_ref, wup_hbm, wdown_hbm, wc_ref, gain_ref, bags_ref, keep_ref, send_ref, tail_ref,
     inv_ref, ds1, ds2, wups, wupr, cot_ref, wup_ref, wdown_ref, sems) = refs[3 + with_ids:]
    copies = [pltpu.make_async_copy(source, target, sems.at[i]) for i, (source, target) in enumerate((
        (wup_hbm, wup_ref), (wdown_hbm, wdown_ref), (cot_hbm.at[pl.ds(part * b, b)], cot_ref)))]
    for copy in copies:
        copy.start()
    for j in range(64):
        inv_ref[fm_ref[j]] = j
    if with_ids:
        for n in range(64):
            v = ids_ref[n]
            rows = jnp.concatenate([jnp.bitwise_and(v, 255), lax.shift_right_logical(v, 8), jnp.zeros((12, 128), jnp.int32)], axis=0)
            bags_ref[inv_ref[n], 64:80, :] = rows.astype(F32).astype(BF)
    x = pooled_ref[...]
    gain = gain_ref[...]
    projt = projt_ref[...]
    wc = wc_ref[...]
    consts = jnp.transpose(jnp.concatenate([wc, projt], axis=0).astype(F32)).astype(BF)
    xcat = jnp.concatenate([x[s] for s in range(b)], axis=1)
    head = dot_nn(jnp.concatenate([projt, wc], axis=0), xcat)
    pts = [head[0:16, s * 128:(s + 1) * 128].astype(BF) for s in range(b)]
    inter = jnp.stack([dot_nt(pts[s], x[s]) for s in range(b)], axis=0)
    inter = jnp.swapaxes(inter, 0, 1)
    inter = jnp.concatenate([inter[k] for k in range(16)], axis=1)
    cen = inter - jnp.mean(inter, axis=1, keepdims=True)
    inv_fm = lax.rsqrt(jnp.mean(cen * cen, axis=1, keepdims=True) + 1e-5)
    normed = cen * inv_fm
    nb = normed.astype(BF)
    copies[0].wait()
    for q in range(4):
        wups[...] = wup_ref[:, q * 128:(q + 1) * 128].astype(F32)
        for k in range(16):
            wupr[k * 64:(k + 1) * 64, q * 128:(q + 1) * 128] = wups[pl.ds(k, 64, stride=16), :].astype(BF)
    preact = dot_nn(nb, wupr[...])
    sig = jax.nn.sigmoid(preact)
    hidden = (preact * sig).astype(BF)
    copies[1].wait()
    fm_out = dot_nn(hidden, wdown_ref[...])
    copies[2].wait()
    gg = jnp.zeros((8, 128), F32)
    dfms = []
    for m in range(32):
        if m % 16 == 0:
            xf = jnp.swapaxes(pooled_ref[:, m:m + 16, :], 0, 1)
            cf = jnp.swapaxes(cot_ref[:, m:m + 16, :], 0, 1)
        dsum, cot_normed = out_norm(
            fm_out[:, m * 128:(m + 1) * 128] + xf[m % 16].astype(F32), cf[m % 16].astype(F32), gain)
        gg += fold8(cot_normed)
        ds1[m] = dsum
        dfms.append(dsum.astype(BF))
    dlcs = []
    for s in range(b):
        dsum, cot_normed = out_norm(
            head[16:48, s * 128:(s + 1) * 128] + x[s, 32:64].astype(F32), cot_ref[s, 32:64, :].astype(F32), gain)
        gg += fold8(cot_normed)
        ds2[s] = dsum
        dlcs.append(dsum.astype(BF))
    dfm = jnp.concatenate(dfms, axis=1)
    hg = dot_nt(dfm, wdown_ref[...])
    dpre = (hg * sig * (1.0 + preact * (1.0 - sig))).astype(BF)
    first_core = core_ref[0] == 0
    for ref, flag in ((keep_ref, first_core), (send_ref, jnp.logical_not(first_core))):
        ref[:, 0:512] = jnp.where(flag, nb[:, 0:512], nb[:, 512:1024])
        ref[:, 512:1024] = dpre
        ref[:, 1024:1280] = jnp.where(flag, hidden[:, 0:256], hidden[:, 256:512])
        ref[:, 1280:5376] = dfm
    dnormed = dot_nt(dpre, wupr[...])
    first = jnp.mean(dnormed, axis=1, keepdims=True)
    second = jnp.mean(dnormed * normed, axis=1, keepdims=True)
    dinter = (inv_fm * (dnormed - first - normed * second)).astype(BF).astype(F32)
    dinter = jnp.swapaxes(jnp.stack([dinter[:, k * 64:(k + 1) * 64] for k in range(16)], axis=0), 0, 1)
    zero = jnp.zeros((16, 128), BF)
    tails = []
    for g in range(b // 16):
        outs = []
        for half in range(2):
            group = [g * 16 + half * 8 + i for i in range(8)]
            for s in group:
                dproj = dot_nn(dinter[s].astype(BF), x[s]).astype(BF)
                tails.append(jnp.concatenate([dlcs[s], dproj], axis=0))
            block = dinter[group[0]:group[0] + 8].reshape(128, 64)
            left = jnp.concatenate([jnp.transpose(block).astype(BF), consts], axis=1)
            right = jnp.concatenate(
                [jnp.concatenate([pts[s] if i == r else zero for i, s in enumerate(group)], axis=1) for r in range(8)]
                + [jnp.concatenate([tails[s] for s in group], axis=1)], axis=0)
            res = dot_nn(left, right)
            outs += [res[:, i * 128:(i + 1) * 128] for i in range(8)]
        for n in range(8):
            rows = [v[n * 8:(n + 1) * 8] for v in outs]
            if n >= 4:
                rows = [v + ds2[g * 16 + i, (n - 4) * 8:(n - 3) * 8, :] for i, v in enumerate(rows)]
            turned = jnp.swapaxes(jnp.stack(rows, axis=0), 0, 1)
            for i in range(8):
                v = turned[i]
                if n < 4:
                    v = v + ds1[n * 8 + i, g * 16:(g + 1) * 16, :]
                bags_ref[inv_ref[n * 8 + i], g * 16:(g + 1) * 16, :] = v.astype(BF)
    gsm = dot_nt(jnp.concatenate(tails, axis=1), xcat)
    tail_ref[...] = jnp.concatenate([
        jnp.concatenate([gsm, jnp.zeros((48, 64), F32)], axis=1),
        jnp.broadcast_to(jnp.sum(gg, axis=0, keepdims=True), (16, 128))], axis=0) * scale


def layer_call(part, batch, feature_map, core, pooled, ids, cotangent, projt, w_up, w_down, w_compress, gain, scale):
    full = lambda *sh: pl.BlockSpec(sh, lambda i: (0,) * len(sh))
    scalars = pl.BlockSpec(memory_space=pltpu.SMEM)
    far = pl.BlockSpec(memory_space=pl.ANY)
    with_ids = ids is not None
    depth = batch + 16 if with_ids else batch
    return pl.pallas_call(
        functools.partial(layer_kernel, scale, batch, part, int(with_ids)),
        grid=(1,),
        in_specs=[scalars, scalars, pl.BlockSpec((batch, 64, 128), lambda i: (part, 0, 0))]
        + ([full(64, 2, 128)] if with_ids else [])
        + [far, full(16, 64), far, far, full(32, 64), full(1, 128)],
        out_specs=[full(64, depth, 128), full(batch, 5376), full(batch, 5376), full(64, 128)],
        out_shape=[jax.ShapeDtypeStruct((64, depth, 128), BF),
                   jax.ShapeDtypeStruct((batch, 5376), BF),
                   jax.ShapeDtypeStruct((batch, 5376), BF),
                   jax.ShapeDtypeStruct((64, 128), F32)],
        scratch_shapes=[pltpu.SMEM((64,), jnp.int32),
                        pltpu.VMEM((32, batch, 128), F32), pltpu.VMEM((batch, 32, 128), F32),
                        pltpu.VMEM((1024, 128), F32), pltpu.VMEM((1024, 512), BF),
                        pltpu.VMEM((batch, 64, 128), BF), pltpu.VMEM((1024, 512), BF), pltpu.VMEM((512, 4096), BF),
                        pltpu.SemaphoreType.DMA((3,))],
        compiler_params=pltpu.CompilerParams(vmem_limit_bytes=VMEM_BYTES),
        cost_estimate=pl.CostEstimate(flops=15 * 10**9, bytes_accessed=10 << 20, transcendentals=0),
        name="layer_first" if with_ids else "layer_second",
    )(*([feature_map, core, pooled] + ([ids] if with_ids else [])
        + [cotangent, projt, w_up, w_down, w_compress, gain]))


def weight_kernel(scale, a0_ref, b0_ref, a1_ref, b1_ref, tail0_ref, tail1_ref, w_ref, gus):
    acts = jnp.concatenate([a0_ref[...], b0_ref[...], a1_ref[...], b1_ref[...]], axis=0)
    tail = tail0_ref[...] + tail1_ref[...]
    tail = jnp.concatenate([tail[q * 16:(q + 1) * 16, :] for q in range(4)], axis=1).astype(BF)
    up = dot_tn(acts[:, 0:512], acts[:, 512:1024]) * scale
    for q in range(4):
        for k in range(8):
            gus[pl.ds(k, 64, stride=8), :] = up[k * 64:(k + 1) * 64, q * 128:(q + 1) * 128]
        for z in range(8):
            w_ref[z, 0:64, q * 128:(q + 1) * 128] = gus[z * 64:(z + 1) * 64, :].astype(BF)
    hid = acts[:, 1024:1280]
    for q in range(8):
        down = (dot_tn(hid, acts[:, 1280 + q * 512:1792 + q * 512]) * scale).astype(BF)
        for z in range(8):
            w_ref[z, 64 + q * 32:96 + q * 32, :] = down[z * 32:(z + 1) * 32, :]
    for z in range(8):
        w_ref[z, 320:336, :] = tail


def weight_call(acts, tails, scale):
    return pl.pallas_call(
        functools.partial(weight_kernel, scale),
        out_shape=jax.ShapeDtypeStruct((8, 336, 512), BF),
        scratch_shapes=[pltpu.VMEM((512, 128), F32)],
        compiler_params=pltpu.CompilerParams(vmem_limit_bytes=VMEM_BYTES),
        cost_estimate=pl.CostEstimate(flops=3 * 10**9, bytes_accessed=6 << 20, transcendentals=0),
        name="weight_grads",
    )(*acts, *tails)


def table_kernel(pairs, last, *refs):
    if last:
        ids_ref, bags_ref, start_ref, out_ref, acc = refs
    else:
        ids_ref, bags_ref, acc = refs
        acc = acc.at[0]
    step = pl.program_id(1)
    side = slice(64, 128) if last else slice(0, 64)
    ids = []
    for i in range(pairs):
        codes = ids_ref[i, :, 0].astype(F32)
        codes = codes[:, 0:2] + 256.0 * codes[:, 2:4]
        ids.append(jnp.concatenate([codes[0][:, side], codes[1][:, side]], axis=1))
    ids = jnp.concatenate(ids, axis=0).astype(jnp.int32)
    low = jnp.transpose(lax.shift_right_logical(ids, 10).astype(F32), (1, 0))
    high = jnp.bitwise_and(ids, 1023).astype(jnp.int16)
    iota = lax.broadcasted_iota(jnp.int16, (1024, 128), 0)
    left, right = [], []
    for i in range(pairs):
        values = bags_ref[i, :, 0].reshape(128, 128)
        for t in range(2):
            r = 2 * i + t
            left.append(jnp.where(iota == high[r:r + 1, :], jnp.bfloat16(1), jnp.bfloat16(0)))
            column = jnp.broadcast_to(low[:, r:r + 1], (128, 128)).astype(BF)
            right.append(jnp.concatenate(
                [jnp.where(column == jnp.bfloat16(q), values, jnp.bfloat16(0)) for q in range(4)], axis=1))
    part = jnp.dot(jnp.concatenate(left, axis=1), jnp.concatenate(right, axis=0), preferred_element_type=F32)

    @pl.when(step == 0)
    def _():
        acc[...] = start_ref[0] + part if last else part

    @pl.when(step > 0)
    def _():
        acc[...] += part

    if last:
        @pl.when(step == pl.num_programs(1) - 1)
        def _():
            for q in range(4):
                for h in range(2):
                    out_ref[h * 4 + q, 0] = acc[h * 512:(h + 1) * 512, q * 128:(q + 1) * 128].astype(BF)


def table_call(ids, bags, start=None, pairs=16):
    last = start is not None
    sums = pl.BlockSpec((1, 1024, 512), lambda j, i: (j, 0, 0))
    return pl.pallas_call(
        functools.partial(table_kernel, pairs, last),
        grid=(2, ids.shape[0] // pairs),
        in_specs=[pl.BlockSpec((pairs, 2, 1, 16, 128), lambda j, i: (i, 0, j, 4, 0)),
                  pl.BlockSpec((pairs, 2, 1, 64, 128), lambda j, i: (i, 0, j, 0, 0))] + ([sums] if last else []),
        out_specs=pl.BlockSpec((8, 1, 512, 128), lambda j, i: (0, j, 0, 0)) if last else sums,
        out_shape=jax.ShapeDtypeStruct((8, 2, 512, 128), BF) if last else jax.ShapeDtypeStruct((2, 1024, 512), F32),
        scratch_shapes=[pltpu.VMEM((1024, 512), F32)] if last else [],
        compiler_params=pltpu.CompilerParams(vmem_limit_bytes=VMEM_BYTES),
        cost_estimate=pl.CostEstimate(flops=9 * 10**9, bytes_accessed=5 << 20, transcendentals=0),
        name="table_last" if last else "table_first",
    )(*([ids, bags] + ([start] if last else [])))


AXES = ("y", "zh", "x", "zl", "c")
HST = ("y", "zh", "x")
LOCAL = ("zl", "c")
SIZES = (4, 2, 4, 4, 2)
PLANE = ("y", "c", "x")


def weight_moves():
    up, down = [], []
    for d in range(256):
        y, zh, x, zl, c = (d // 64, d // 32 % 2, d // 8 % 4, d // 2 % 4, d % 2)
        z, sub = zh * 4 + zl, y * 4 + x
        up.append((d, z * 32 + (sub // 2) * 4 + 2 * c + sub % 2))
        down.append((d, c * 128 + z * 16 + sub))
    return up, down


def shards(pooled, cotangent, projection, w_up, w_down, w_compress, ln_gain, feature_map, bag_row_index):
    batch = pooled.shape[0] // 2
    scale = float(batch * 512) ** (-0.5)
    core = lax.axis_index("c").astype(jnp.int32).reshape(1)
    ids = jnp.transpose(bag_row_index, (1, 2, 0))
    swap = [(0, 1), (1, 0)]

    def layer(part):
        return layer_call(part, batch, feature_map, core, pooled, ids if part == 0 else None, cotangent,
                          projection.T, w_up, w_down, w_compress, ln_gain.reshape(1, 128), scale)

    def exchange(bag):
        return lax.all_to_all(bag, PLANE, 0, 0, tiled=True)

    bag0, keep0, send0, tail0 = layer(0)
    first = exchange(bag0)
    bag1, keep1, send1, tail1 = layer(1)
    send1, first = lax.optimization_barrier((send1, first))
    acts = (keep0, lax.ppermute(send0, "c", swap), keep1, lax.ppermute(send1, "c", swap))
    weights = weight_call(acts, (tail0, tail1), scale)
    bag1, weights = lax.optimization_barrier((bag1, weights))
    weights = lax.psum_scatter(weights.reshape(8 * 336, 512), ("zh", "zl"), scatter_dimension=0, tiled=True)
    second = exchange(bag1)
    first = first.reshape(16, 2, 2, batch + 16, 128)
    rows = table_call(first, first)
    rows = table_call(first, second.reshape(16, 2, 2, batch, 128), rows)
    weights, _ = lax.optimization_barrier((weights, rows))
    rows = lax.psum_scatter(rows.reshape(8192, 128), ("zh", "zl"), scatter_dimension=0, tiled=True)
    pieces = jnp.concatenate(
        [weights[0:64].reshape(16, 4, 512),
         weights[64:320].reshape(8, 16, 2, 512).transpose(1, 0, 2, 3).reshape(16, 16, 512),
         jnp.broadcast_to(weights[320:336], (16, 16, 512))], axis=1)
    pieces = lax.all_to_all(pieces, ("y", "x"), 0, 0, tiled=True)
    total = jnp.sum(pieces.astype(F32), axis=0)
    up_moves, down_moves = weight_moves()
    gu = lax.ppermute(total[0:4], AXES, up_moves)
    gd = lax.ppermute(total[4:20], AXES, down_moves).reshape(8, 2, 512).transpose(1, 0, 2).reshape(2, 4096)
    tail = total[20:36].reshape(16, 4, 128).transpose(1, 0, 2).reshape(64, 128)
    tail = tail + lax.ppermute(tail, "c", swap)
    small = (tail[32:48, :64].T, tail[:32, :64], tail[48])
    rows, gu, gd, small = lax.optimization_barrier((rows, gu, gd, small))
    table_grad = lax.ppermute(rows, ("zh", "c"), [(0, 0), (1, 2), (2, 1), (3, 3)]).astype(F32)
    return (table_grad.reshape(2, 512, 128), gu, gd) + tuple(small)


def solution(mesh):
    inner = Mesh(mesh.devices.reshape(SIZES), AXES)
    split = P(AXES, None, None)
    return jax.shard_map(
        shards,
        mesh=inner,
        in_specs=(split, split, P(), P(), P(), P(), P(), P(), split),
        out_specs=(P(HST, LOCAL, None), P(AXES, None), P(AXES, None), P(), P(), P()),
        check_vma=False,
    )
```

```python
import functools

import jax
import jax.numpy as jnp
from jax import lax
from jax.experimental import pallas as pl
from jax.experimental.pallas import tpu as pltpu
from jax.sharding import Mesh
from jax.sharding import PartitionSpec as P

BF, F32 = jnp.bfloat16, jnp.float32
VMEM_BYTES = 60 << 20


def dot_nn(a, b):
    return lax.dot_general(a, b, (((1,), (0,)), ((), ())), preferred_element_type=F32)


def dot_nt(a, b):
    return lax.dot_general(a, b, (((1,), (1,)), ((), ())), preferred_element_type=F32)


def dot_tn(a, b):
    return lax.dot_general(a, b, (((0,), (0,)), ((), ())), preferred_element_type=F32)


def out_norm(summed, cot, gain):
    centered = summed - jnp.mean(summed, axis=-1, keepdims=True)
    inverse = lax.rsqrt(jnp.mean(centered * centered, axis=-1, keepdims=True) + 1e-5)
    normed = centered * inverse
    cot_normed = cot * normed
    dnorm = cot * gain
    first = jnp.mean(dnorm, axis=-1, keepdims=True)
    second = jnp.mean(cot_normed * gain, axis=-1, keepdims=True)
    return inverse * (dnorm - first - normed * second), cot_normed


def fold8(v):
    return jnp.sum(v.reshape(v.shape[0] // 8, 8, 128), axis=0)


def layer_kernel(scale, b, part, with_ids, *refs):
    fm_ref, core_ref, pooled_ref = refs[:3]
    ids_ref = refs[3] if with_ids else None
    (cot_hbm, projt_ref, wup_hbm, wdown_hbm, wc_ref, gain_ref, bags_ref, keep_ref, send_ref, tail_ref,
     inv_ref, ds1, ds2, wups, wupr, cot_ref, wup_ref, wdown_ref, sems) = refs[3 + with_ids:]
    copies = [pltpu.make_async_copy(source, target, sems.at[i]) for i, (source, target) in enumerate((
        (wup_hbm, wup_ref), (wdown_hbm, wdown_ref), (cot_hbm.at[pl.ds(part * b, b)], cot_ref)))]
    for copy in copies:
        copy.start()
    for j in range(64):
        inv_ref[fm_ref[j]] = j
    if with_ids:
        for n in range(64):
            v = ids_ref[n]
            rows = jnp.concatenate([jnp.bitwise_and(v, 255), lax.shift_right_logical(v, 8), jnp.zeros((12, 128), jnp.int32)], axis=0)
            bags_ref[inv_ref[n], 64:80, :] = rows.astype(F32).astype(BF)
    x = pooled_ref[...]
    gain = gain_ref[...]
    projt = projt_ref[...]
    wc = wc_ref[...]
    consts = jnp.transpose(jnp.concatenate([wc, projt], axis=0).astype(F32)).astype(BF)
    xcat = jnp.concatenate([x[s] for s in range(b)], axis=1)
    head = dot_nn(jnp.concatenate([projt, wc], axis=0), xcat)
    pts = [head[0:16, s * 128:(s + 1) * 128].astype(BF) for s in range(b)]
    inter = jnp.stack([dot_nt(pts[s], x[s]) for s in range(b)], axis=0)
    inter = jnp.swapaxes(inter, 0, 1)
    inter = jnp.concatenate([inter[k] for k in range(16)], axis=1)
    cen = inter - jnp.mean(inter, axis=1, keepdims=True)
    inv_fm = lax.rsqrt(jnp.mean(cen * cen, axis=1, keepdims=True) + 1e-5)
    normed = cen * inv_fm
    nb = normed.astype(BF)
    copies[0].wait()
    for q in range(4):
        wups[...] = wup_ref[:, q * 128:(q + 1) * 128].astype(F32)
        for k in range(16):
            wupr[k * 64:(k + 1) * 64, q * 128:(q + 1) * 128] = wups[pl.ds(k, 64, stride=16), :].astype(BF)
    preact = dot_nn(nb, wupr[...])
    sig = jax.nn.sigmoid(preact)
    hidden = (preact * sig).astype(BF)
    copies[1].wait()
    fm_out = dot_nn(hidden, wdown_ref[...])
    copies[2].wait()
    gg = jnp.zeros((8, 128), F32)
    dfms = []
    for m in range(32):
        if m % 16 == 0:
            xf = jnp.swapaxes(pooled_ref[:, m:m + 16, :], 0, 1)
            cf = jnp.swapaxes(cot_ref[:, m:m + 16, :], 0, 1)
        dsum, cot_normed = out_norm(
            fm_out[:, m * 128:(m + 1) * 128] + xf[m % 16].astype(F32), cf[m % 16].astype(F32), gain)
        gg += fold8(cot_normed)
        ds1[m] = dsum
        dfms.append(dsum.astype(BF))
    dlcs = []
    for s in range(b):
        dsum, cot_normed = out_norm(
            head[16:48, s * 128:(s + 1) * 128] + x[s, 32:64].astype(F32), cot_ref[s, 32:64, :].astype(F32), gain)
        gg += fold8(cot_normed)
        ds2[s] = dsum
        dlcs.append(dsum.astype(BF))
    dfm = jnp.concatenate(dfms, axis=1)
    hg = dot_nt(dfm, wdown_ref[...])
    dpre = (hg * sig * (1.0 + preact * (1.0 - sig))).astype(BF)
    first_core = core_ref[0] == 0
    for ref, flag in ((keep_ref, first_core), (send_ref, jnp.logical_not(first_core))):
        ref[:, 0:512] = jnp.where(flag, nb[:, 0:512], nb[:, 512:1024])
        ref[:, 512:1024] = dpre
        ref[:, 1024:1280] = jnp.where(flag, hidden[:, 0:256], hidden[:, 256:512])
        ref[:, 1280:5376] = dfm
    dnormed = dot_nt(dpre, wupr[...])
    first = jnp.mean(dnormed, axis=1, keepdims=True)
    second = jnp.mean(dnormed * normed, axis=1, keepdims=True)
    dinter = (inv_fm * (dnormed - first - normed * second)).astype(BF).astype(F32)
    dinter = jnp.swapaxes(jnp.stack([dinter[:, k * 64:(k + 1) * 64] for k in range(16)], axis=0), 0, 1)
    zero = jnp.zeros((16, 128), BF)
    tails = []
    for g in range(b // 16):
        outs = []
        for half in range(2):
            group = [g * 16 + half * 8 + i for i in range(8)]
            for s in group:
                dproj = dot_nn(dinter[s].astype(BF), x[s]).astype(BF)
                tails.append(jnp.concatenate([dlcs[s], dproj], axis=0))
            block = dinter[group[0]:group[0] + 8].reshape(128, 64)
            left = jnp.concatenate([jnp.transpose(block).astype(BF), consts], axis=1)
            right = jnp.concatenate(
                [jnp.concatenate([pts[s] if i == r else zero for i, s in enumerate(group)], axis=1) for r in range(8)]
                + [jnp.concatenate([tails[s] for s in group], axis=1)], axis=0)
            res = dot_nn(left, right)
            outs += [res[:, i * 128:(i + 1) * 128] for i in range(8)]
        for n in range(8):
            rows = [v[n * 8:(n + 1) * 8] for v in outs]
            if n >= 4:
                rows = [v + ds2[g * 16 + i, (n - 4) * 8:(n - 3) * 8, :] for i, v in enumerate(rows)]
            turned = jnp.swapaxes(jnp.stack(rows, axis=0), 0, 1)
            for i in range(8):
                v = turned[i]
                if n < 4:
                    v = v + ds1[n * 8 + i, g * 16:(g + 1) * 16, :]
                bags_ref[inv_ref[n * 8 + i], g * 16:(g + 1) * 16, :] = v.astype(BF)
    gsm = dot_nt(jnp.concatenate(tails, axis=1), xcat)
    tail_ref[...] = jnp.concatenate([
        jnp.concatenate([gsm[0:24], gsm[24:48]], axis=1),
        jnp.broadcast_to(jnp.sum(gg, axis=0, keepdims=True), (8, 128))], axis=0) * scale


def layer_call(part, batch, feature_map, core, pooled, ids, cotangent, projt, w_up, w_down, w_compress, gain, scale):
    full = lambda *sh: pl.BlockSpec(sh, lambda i: (0,) * len(sh))
    scalars = pl.BlockSpec(memory_space=pltpu.SMEM)
    far = pl.BlockSpec(memory_space=pl.ANY)
    with_ids = ids is not None
    depth = batch + 16 if with_ids else batch
    return pl.pallas_call(
        functools.partial(layer_kernel, scale, batch, part, int(with_ids)),
        grid=(1,),
        in_specs=[scalars, scalars, pl.BlockSpec((batch, 64, 128), lambda i: (part, 0, 0))]
        + ([full(64, 2, 128)] if with_ids else [])
        + [far, full(16, 64), far, far, full(32, 64), full(1, 128)],
        out_specs=[full(64, depth, 128), full(batch, 5376), full(batch, 5376), full(32, 128)],
        out_shape=[jax.ShapeDtypeStruct((64, depth, 128), BF),
                   jax.ShapeDtypeStruct((batch, 5376), BF),
                   jax.ShapeDtypeStruct((batch, 5376), BF),
                   jax.ShapeDtypeStruct((32, 128), F32)],
        scratch_shapes=[pltpu.SMEM((64,), jnp.int32),
                        pltpu.VMEM((32, batch, 128), F32), pltpu.VMEM((batch, 32, 128), F32),
                        pltpu.VMEM((1024, 128), F32), pltpu.VMEM((1024, 512), BF),
                        pltpu.VMEM((batch, 64, 128), BF), pltpu.VMEM((1024, 512), BF), pltpu.VMEM((512, 4096), BF),
                        pltpu.SemaphoreType.DMA((3,))],
        compiler_params=pltpu.CompilerParams(vmem_limit_bytes=VMEM_BYTES),
        cost_estimate=pl.CostEstimate(flops=15 * 10**9, bytes_accessed=10 << 20, transcendentals=0),
        name="layer_first" if with_ids else "layer_second",
    )(*([feature_map, core, pooled] + ([ids] if with_ids else [])
        + [cotangent, projt, w_up, w_down, w_compress, gain]))


def weight_kernel(scale, a0_ref, b0_ref, a1_ref, b1_ref, tail0_ref, tail1_ref, w_ref, gus):
    acts = jnp.concatenate([a0_ref[...], b0_ref[...], a1_ref[...], b1_ref[...]], axis=0)
    tail = tail0_ref[...] + tail1_ref[...]
    tail = jnp.concatenate([tail[q * 8:(q + 1) * 8, :] for q in range(4)], axis=1)
    tail = jnp.concatenate([tail, jnp.zeros((8, 512), F32)], axis=0).astype(BF)
    up = dot_tn(acts[:, 0:512], acts[:, 512:1024]) * scale
    for q in range(4):
        for k in range(8):
            gus[pl.ds(k, 64, stride=8), :] = up[k * 64:(k + 1) * 64, q * 128:(q + 1) * 128]
        for z in range(4):
            w_ref[z, 0:128, q * 128:(q + 1) * 128] = gus[z * 128:(z + 1) * 128, :].astype(BF)
    hid = acts[:, 1024:1280]
    for q in range(8):
        down = (dot_tn(hid, acts[:, 1280 + q * 512:1792 + q * 512]) * scale).astype(BF)
        for z in range(4):
            w_ref[z, 128 + q * 64:192 + q * 64, :] = down[z * 64:(z + 1) * 64, :]
    for z in range(4):
        w_ref[z, 640:656, :] = tail


def weight_call(acts, tails, scale):
    return pl.pallas_call(
        functools.partial(weight_kernel, scale),
        out_shape=jax.ShapeDtypeStruct((4, 656, 512), BF),
        scratch_shapes=[pltpu.VMEM((512, 128), F32)],
        compiler_params=pltpu.CompilerParams(vmem_limit_bytes=VMEM_BYTES),
        cost_estimate=pl.CostEstimate(flops=3 * 10**9, bytes_accessed=6 << 20, transcendentals=0),
        name="weight_grads",
    )(*acts, *tails)


def table_kernel(pairs, group, parts, last, *refs):
    span = 4096 // parts
    if last:
        ids_ref, bags_ref, start_ref, out_ref, acc = refs
    else:
        ids_ref, bags_ref, acc = refs
        acc = acc.at[0]
    side = slice(64, 128) if last else slice(0, 64)
    ids = []
    for i in range(pairs):
        codes = ids_ref[i, :, 0].astype(F32)
        codes = codes[:, 0:2] + 256.0 * codes[:, 2:4]
        ids.append(jnp.concatenate([codes[0][:, side], codes[1][:, side]], axis=1))
    ids = jnp.concatenate(ids, axis=0).astype(jnp.int32)
    low = jnp.transpose(lax.shift_right_logical(ids, span.bit_length() - 1).astype(F32), (1, 0))
    high = jnp.bitwise_and(ids, span - 1).astype(jnp.int16)
    iota = lax.broadcasted_iota(jnp.int16, (span, 128), 0)
    for g in range(pairs // group):
        left, right = [], []
        for i in range(g * group, (g + 1) * group):
            values = bags_ref[i, :, 0].reshape(128, 128)
            for t in range(2):
                r = 2 * i + t
                left.append(jnp.where(iota == high[r:r + 1, :], jnp.bfloat16(1), jnp.bfloat16(0)))
                column = jnp.broadcast_to(low[:, r:r + 1], (128, 128)).astype(BF)
                right.append(jnp.concatenate(
                    [jnp.where(column == jnp.bfloat16(q), values, jnp.bfloat16(0)) for q in range(parts)], axis=1))
        part = jnp.dot(jnp.concatenate(left, axis=1), jnp.concatenate(right, axis=0), preferred_element_type=F32)
        if g == 0:
            acc[...] = start_ref[0] + part if last else part
        else:
            acc[...] += part

    if last:
        for p in range(8):
            q, h = p // (8 // parts), p % (8 // parts)
            out_ref[(p % 2) * 4 + p // 2, 0] = acc[h * 512:(h + 1) * 512, q * 128:(q + 1) * 128].astype(BF)


def table_call(ids, bags, start=None, pairs=16, group=4, parts=4):
    last = start is not None
    sums = pl.BlockSpec((1, 4096 // parts, 128 * parts), lambda j, i: (j, 0, 0))
    return pl.pallas_call(
        functools.partial(table_kernel, pairs, group, parts, last),
        grid=(2, ids.shape[0] // pairs),
        in_specs=[pl.BlockSpec((pairs, 2, 1, 16, 128), lambda j, i: (i, 0, j, 4, 0)),
                  pl.BlockSpec((pairs, 2, 1, 64, 128), lambda j, i: (i, 0, j, 0, 0))] + ([sums] if last else []),
        out_specs=pl.BlockSpec((8, 1, 512, 128), lambda j, i: (0, j, 0, 0)) if last else sums,
        out_shape=jax.ShapeDtypeStruct((8, 2, 512, 128), BF) if last else jax.ShapeDtypeStruct((2, 4096 // parts, 128 * parts), F32),
        scratch_shapes=[pltpu.VMEM((4096 // parts, 128 * parts), F32)] if last else [],
        compiler_params=pltpu.CompilerParams(vmem_limit_bytes=VMEM_BYTES),
        cost_estimate=pl.CostEstimate(flops=9 * 10**9, bytes_accessed=5 << 20, transcendentals=0),
        name="table_last" if last else "table_first",
    )(*([ids, bags] + ([start] if last else [])))


AXES = ("y", "zh", "x", "zl", "c")
HST = ("y", "zh", "x")
LOCAL = ("zl", "c")
SIZES = (4, 2, 4, 4, 2)
PLANE = ("y", "c", "x")


def weight_moves():
    up, down = [], []
    for d in range(256):
        y, zh, x, zl, c = (d // 64, d // 32 % 2, d // 8 % 4, d // 2 % 4, d % 2)
        unit = zl * 32 + (y * 2 + zh) * 4 + x
        up.append((d, (unit // 2) * 4 + 2 * c + unit % 2))
        down.append((d, c * 128 + unit))
    return up, down


def shards(pooled, cotangent, projection, w_up, w_down, w_compress, ln_gain, feature_map, bag_row_index):
    batch = pooled.shape[0] // 2
    scale = float(batch * 512) ** (-0.5)
    core = lax.axis_index("c").astype(jnp.int32).reshape(1)
    ids = jnp.transpose(bag_row_index, (1, 2, 0))
    swap = [(0, 1), (1, 0)]

    def layer(part):
        return layer_call(part, batch, feature_map, core, pooled, ids if part == 0 else None, cotangent,
                          projection.T, w_up, w_down, w_compress, ln_gain.reshape(1, 128), scale)

    def exchange(bag):
        return lax.all_to_all(bag, PLANE, 0, 0, tiled=True)

    bag0, keep0, send0, tail0 = layer(0)
    first = exchange(bag0)
    bag1, keep1, send1, tail1 = layer(1)
    acts = (keep0, lax.ppermute(send0, "c", swap), keep1, lax.ppermute(send1, "c", swap))
    weights = weight_call(acts, (tail0, tail1), scale)
    bag1, weights, first = lax.optimization_barrier((bag1, weights, first))
    weights = lax.psum_scatter(weights.reshape(4 * 656, 512), "zl", scatter_dimension=0, tiled=True)
    second = exchange(bag1)
    first = first.reshape(16, 2, 2, batch + 16, 128)
    rows = table_call(first, first)
    rows = table_call(first, second.reshape(16, 2, 2, batch, 128), rows)
    weights, _ = lax.optimization_barrier((weights, rows))
    rows = lax.psum_scatter(rows.reshape(8192, 128), ("zh", "zl"), scatter_dimension=0, tiled=True)
    pieces = jnp.concatenate(
        [weights[0:128].reshape(32, 4, 512),
         weights[128:640].reshape(8, 32, 2, 512).transpose(1, 0, 2, 3).reshape(32, 16, 512),
         jnp.broadcast_to(weights[640:648], (32, 8, 512))], axis=1)
    pieces = lax.all_to_all(pieces, HST, 0, 0, tiled=True)
    total = jnp.sum(pieces.astype(F32), axis=0)
    up_moves, down_moves = weight_moves()
    gu = lax.ppermute(total[0:4], AXES, up_moves)
    gd = lax.ppermute(total[4:20], AXES, down_moves).reshape(8, 2, 512).transpose(1, 0, 2).reshape(2, 4096)
    tail = total[20:28].reshape(8, 4, 128).transpose(1, 0, 2).reshape(32, 128)
    tail = tail + lax.ppermute(tail, "c", swap)
    both = jnp.concatenate([tail[0:24, :64], tail[0:24, 64:]], axis=0)
    small = (both[32:48].T, both[0:32], tail[24])
    rows, gu, gd, small = lax.optimization_barrier((rows, gu, gd, small))
    table_grad = lax.ppermute(rows, ("zh", "c"), [(0, 0), (1, 2), (2, 1), (3, 3)]).astype(F32)
    return (table_grad.reshape(2, 512, 128), gu, gd) + tuple(small)


def solution(mesh):
    inner = Mesh(mesh.devices.reshape(SIZES), AXES)
    split = P(AXES, None, None)
    return jax.shard_map(
        shards,
        mesh=inner,
        in_specs=(split, split, P(), P(), P(), P(), P(), P(), split),
        out_specs=(P(HST, LOCAL, None), P(AXES, None), P(AXES, None), P(), P(), P()),
        check_vma=False,
    )
```

```python
import functools

import jax
import jax.numpy as jnp
from jax import lax
from jax.experimental import pallas as pl
from jax.experimental.pallas import tpu as pltpu
from jax.sharding import Mesh
from jax.sharding import PartitionSpec as P

BF, F32 = jnp.bfloat16, jnp.float32
VMEM_BYTES = 60 << 20


def dot_nn(a, b):
    return lax.dot_general(a, b, (((1,), (0,)), ((), ())), preferred_element_type=F32)


def dot_nt(a, b):
    return lax.dot_general(a, b, (((1,), (1,)), ((), ())), preferred_element_type=F32)


def dot_tn(a, b):
    return lax.dot_general(a, b, (((0,), (0,)), ((), ())), preferred_element_type=F32)


def out_norm(summed, cot, gain):
    centered = summed - jnp.mean(summed, axis=-1, keepdims=True)
    inverse = lax.rsqrt(jnp.mean(centered * centered, axis=-1, keepdims=True) + 1e-5)
    normed = centered * inverse
    cot_normed = cot * normed
    dnorm = cot * gain
    first = jnp.mean(dnorm, axis=-1, keepdims=True)
    second = jnp.mean(cot_normed * gain, axis=-1, keepdims=True)
    return inverse * (dnorm - first - normed * second), cot_normed


def fold8(v):
    return jnp.sum(v.reshape(v.shape[0] // 8, 8, 128), axis=0)


def layer_kernel(scale, b, part, with_ids, *refs):
    fm_ref, core_ref, pooled_ref = refs[:3]
    ids_ref = refs[3] if with_ids else None
    (cot_hbm, projt_ref, wup_hbm, wdown_hbm, wc_ref, gain_ref, bags_ref, keep_ref, send_ref, tail_ref,
     inv_ref, ds1, ds2, wups, wupr, cot_ref, wup_ref, wdown_ref, sems) = refs[3 + with_ids:]
    copies = [pltpu.make_async_copy(source, target, sems.at[i]) for i, (source, target) in enumerate((
        (wup_hbm, wup_ref), (wdown_hbm, wdown_ref), (cot_hbm.at[pl.ds(part * b, b)], cot_ref)))]
    for copy in copies:
        copy.start()
    for j in range(64):
        inv_ref[fm_ref[j]] = j
    if with_ids:
        for n in range(64):
            v = ids_ref[n]
            rows = jnp.concatenate([jnp.bitwise_and(v, 255), lax.shift_right_logical(v, 8), jnp.zeros((12, 128), jnp.int32)], axis=0)
            bags_ref[inv_ref[n], 64:80, :] = rows.astype(F32).astype(BF)
    x = pooled_ref[...]
    gain = gain_ref[...]
    projt = projt_ref[...]
    wc = wc_ref[...]
    consts = jnp.transpose(jnp.concatenate([wc, projt], axis=0).astype(F32)).astype(BF)
    xcat = jnp.concatenate([x[s] for s in range(b)], axis=1)
    head = dot_nn(jnp.concatenate([projt, wc], axis=0), xcat)
    pts = [head[0:16, s * 128:(s + 1) * 128].astype(BF) for s in range(b)]
    inter = jnp.stack([dot_nt(pts[s], x[s]) for s in range(b)], axis=0)
    inter = jnp.swapaxes(inter, 0, 1)
    inter = jnp.concatenate([inter[k] for k in range(16)], axis=1)
    cen = inter - jnp.mean(inter, axis=1, keepdims=True)
    inv_fm = lax.rsqrt(jnp.mean(cen * cen, axis=1, keepdims=True) + 1e-5)
    normed = cen * inv_fm
    nb = normed.astype(BF)
    copies[0].wait()
    for q in range(4):
        wups[...] = wup_ref[:, q * 128:(q + 1) * 128].astype(F32)
        for k in range(16):
            wupr[k * 64:(k + 1) * 64, q * 128:(q + 1) * 128] = wups[pl.ds(k, 64, stride=16), :].astype(BF)
    preact = dot_nn(nb, wupr[...])
    sig = jax.nn.sigmoid(preact)
    hidden = (preact * sig).astype(BF)
    copies[1].wait()
    fm_out = dot_nn(hidden, wdown_ref[...])
    copies[2].wait()
    gg = jnp.zeros((8, 128), F32)
    dfms = []
    for m in range(32):
        if m % 16 == 0:
            xf = jnp.swapaxes(pooled_ref[:, m:m + 16, :], 0, 1)
            cf = jnp.swapaxes(cot_ref[:, m:m + 16, :], 0, 1)
        dsum, cot_normed = out_norm(
            fm_out[:, m * 128:(m + 1) * 128] + xf[m % 16].astype(F32), cf[m % 16].astype(F32), gain)
        gg += fold8(cot_normed)
        ds1[m] = dsum
        dfms.append(dsum.astype(BF))
    dlcs = []
    for s in range(b):
        dsum, cot_normed = out_norm(
            head[16:48, s * 128:(s + 1) * 128] + x[s, 32:64].astype(F32), cot_ref[s, 32:64, :].astype(F32), gain)
        gg += fold8(cot_normed)
        ds2[s] = dsum
        dlcs.append(dsum.astype(BF))
    dfm = jnp.concatenate(dfms, axis=1)
    hg = dot_nt(dfm, wdown_ref[...])
    dpre = (hg * sig * (1.0 + preact * (1.0 - sig))).astype(BF)
    first_core = core_ref[0] == 0
    for ref, flag in ((keep_ref, first_core), (send_ref, jnp.logical_not(first_core))):
        ref[:, 0:512] = jnp.where(flag, nb[:, 0:512], nb[:, 512:1024])
        ref[:, 512:1024] = dpre
        ref[:, 1024:1280] = jnp.where(flag, hidden[:, 0:256], hidden[:, 256:512])
        ref[:, 1280:5376] = dfm
    dnormed = dot_nt(dpre, wupr[...])
    first = jnp.mean(dnormed, axis=1, keepdims=True)
    second = jnp.mean(dnormed * normed, axis=1, keepdims=True)
    dinter = (inv_fm * (dnormed - first - normed * second)).astype(BF).astype(F32)
    dinter = jnp.swapaxes(jnp.stack([dinter[:, k * 64:(k + 1) * 64] for k in range(16)], axis=0), 0, 1)
    zero = jnp.zeros((16, 128), BF)
    tails = []
    for g in range(b // 16):
        outs = []
        for half in range(2):
            group = [g * 16 + half * 8 + i for i in range(8)]
            for s in group:
                dproj = dot_nn(dinter[s].astype(BF), x[s]).astype(BF)
                tails.append(jnp.concatenate([dlcs[s], dproj], axis=0))
            block = dinter[group[0]:group[0] + 8].reshape(128, 64)
            left = jnp.concatenate([jnp.transpose(block).astype(BF), consts], axis=1)
            right = jnp.concatenate(
                [jnp.concatenate([pts[s] if i == r else zero for i, s in enumerate(group)], axis=1) for r in range(8)]
                + [jnp.concatenate([tails[s] for s in group], axis=1)], axis=0)
            res = dot_nn(left, right)
            outs += [res[:, i * 128:(i + 1) * 128] for i in range(8)]
        for n in range(8):
            rows = [v[n * 8:(n + 1) * 8] for v in outs]
            if n >= 4:
                rows = [v + ds2[g * 16 + i, (n - 4) * 8:(n - 3) * 8, :] for i, v in enumerate(rows)]
            turned = jnp.swapaxes(jnp.stack(rows, axis=0), 0, 1)
            for i in range(8):
                v = turned[i]
                if n < 4:
                    v = v + ds1[n * 8 + i, g * 16:(g + 1) * 16, :]
                bags_ref[inv_ref[n * 8 + i], g * 16:(g + 1) * 16, :] = v.astype(BF)
    gsm = dot_nt(jnp.concatenate(tails, axis=1), xcat)
    tail_ref[...] = jnp.concatenate([
        jnp.concatenate([gsm[0:24], gsm[24:48]], axis=1),
        jnp.broadcast_to(jnp.sum(gg, axis=0, keepdims=True), (8, 128))], axis=0) * scale


def layer_call(part, batch, feature_map, core, pooled, ids, cotangent, projt, w_up, w_down, w_compress, gain, scale):
    full = lambda *sh: pl.BlockSpec(sh, lambda i: (0,) * len(sh))
    scalars = pl.BlockSpec(memory_space=pltpu.SMEM)
    far = pl.BlockSpec(memory_space=pl.ANY)
    with_ids = ids is not None
    depth = batch + 16 if with_ids else batch
    return pl.pallas_call(
        functools.partial(layer_kernel, scale, batch, part, int(with_ids)),
        grid=(1,),
        in_specs=[scalars, scalars, pl.BlockSpec((batch, 64, 128), lambda i: (part, 0, 0))]
        + ([full(64, 2, 128)] if with_ids else [])
        + [far, full(16, 64), far, far, full(32, 64), full(1, 128)],
        out_specs=[full(64, depth, 128), full(batch, 5376), full(batch, 5376), full(32, 128)],
        out_shape=[jax.ShapeDtypeStruct((64, depth, 128), BF),
                   jax.ShapeDtypeStruct((batch, 5376), BF),
                   jax.ShapeDtypeStruct((batch, 5376), BF),
                   jax.ShapeDtypeStruct((32, 128), F32)],
        scratch_shapes=[pltpu.SMEM((64,), jnp.int32),
                        pltpu.VMEM((32, batch, 128), F32), pltpu.VMEM((batch, 32, 128), F32),
                        pltpu.VMEM((1024, 128), F32), pltpu.VMEM((1024, 512), BF),
                        pltpu.VMEM((batch, 64, 128), BF), pltpu.VMEM((1024, 512), BF), pltpu.VMEM((512, 4096), BF),
                        pltpu.SemaphoreType.DMA((3,))],
        compiler_params=pltpu.CompilerParams(vmem_limit_bytes=VMEM_BYTES),
        cost_estimate=pl.CostEstimate(flops=15 * 10**9, bytes_accessed=10 << 20, transcendentals=0),
        name="layer_first" if with_ids else "layer_second",
    )(*([feature_map, core, pooled] + ([ids] if with_ids else [])
        + [cotangent, projt, w_up, w_down, w_compress, gain]))


def weight_kernel(scale, a0_ref, b0_ref, a1_ref, b1_ref, tail0_ref, tail1_ref, w_ref, gus):
    acts = jnp.concatenate([a0_ref[...], b0_ref[...], a1_ref[...], b1_ref[...]], axis=0)
    tail = tail0_ref[...] + tail1_ref[...]
    tail = jnp.concatenate([tail[q * 8:(q + 1) * 8, :] for q in range(4)], axis=1)
    tail = jnp.concatenate([tail, jnp.zeros((8, 512), F32)], axis=0).astype(BF)
    up = dot_tn(acts[:, 0:512], acts[:, 512:1024]) * scale
    for q in range(4):
        for k in range(8):
            gus[pl.ds(k, 64, stride=8), :] = up[k * 64:(k + 1) * 64, q * 128:(q + 1) * 128]
        for z in range(8):
            w_ref[z, 0:64, q * 128:(q + 1) * 128] = gus[z * 64:(z + 1) * 64, :].astype(BF)
    hid = acts[:, 1024:1280]
    for q in range(8):
        down = (dot_tn(hid, acts[:, 1280 + q * 512:1792 + q * 512]) * scale).astype(BF)
        for z in range(8):
            w_ref[z, 64 + q * 32:96 + q * 32, :] = down[z * 32:(z + 1) * 32, :]
    for z in range(8):
        w_ref[z, 320:336, :] = tail


def weight_call(acts, tails, scale):
    return pl.pallas_call(
        functools.partial(weight_kernel, scale),
        out_shape=jax.ShapeDtypeStruct((8, 336, 512), BF),
        scratch_shapes=[pltpu.VMEM((512, 128), F32)],
        compiler_params=pltpu.CompilerParams(vmem_limit_bytes=VMEM_BYTES),
        cost_estimate=pl.CostEstimate(flops=3 * 10**9, bytes_accessed=6 << 20, transcendentals=0),
        name="weight_grads",
    )(*acts, *tails)


def table_kernel(pairs, group, parts, last, *refs):
    span = 4096 // parts
    if last:
        ids_ref, bags_ref, start_ref, out_ref, acc = refs
    else:
        ids_ref, bags_ref, acc = refs
        acc = acc.at[0]
    side = slice(64, 128) if last else slice(0, 64)
    ids = []
    for i in range(pairs):
        codes = ids_ref[i, :, 0].astype(F32)
        codes = codes[:, 0:2] + 256.0 * codes[:, 2:4]
        ids.append(jnp.concatenate([codes[0][:, side], codes[1][:, side]], axis=1))
    ids = jnp.concatenate(ids, axis=0).astype(jnp.int32)
    low = jnp.transpose(lax.shift_right_logical(ids, span.bit_length() - 1).astype(F32), (1, 0))
    high = jnp.bitwise_and(ids, span - 1).astype(jnp.int16)
    iota = lax.broadcasted_iota(jnp.int16, (span, 128), 0)
    for g in range(pairs // group):
        left, right = [], []
        for i in range(g * group, (g + 1) * group):
            values = bags_ref[i, :, 0].reshape(128, 128)
            for t in range(2):
                r = 2 * i + t
                left.append(jnp.where(iota == high[r:r + 1, :], jnp.bfloat16(1), jnp.bfloat16(0)))
                column = jnp.broadcast_to(low[:, r:r + 1], (128, 128)).astype(BF)
                right.append(jnp.concatenate(
                    [jnp.where(column == jnp.bfloat16(q), values, jnp.bfloat16(0)) for q in range(parts)], axis=1))
        part = jnp.dot(jnp.concatenate(left, axis=1), jnp.concatenate(right, axis=0), preferred_element_type=F32)
        if g == 0:
            acc[...] = start_ref[0] + part if last else part
        else:
            acc[...] += part

    if last:
        for p in range(8):
            q, h = p // (8 // parts), p % (8 // parts)
            out_ref[(p % 2) * 4 + p // 2, 0] = acc[h * 512:(h + 1) * 512, q * 128:(q + 1) * 128].astype(BF)


def table_call(ids, bags, start=None, pairs=16, group=4, parts=4):
    last = start is not None
    sums = pl.BlockSpec((1, 4096 // parts, 128 * parts), lambda j, i: (j, 0, 0))
    return pl.pallas_call(
        functools.partial(table_kernel, pairs, group, parts, last),
        grid=(2, ids.shape[0] // pairs),
        in_specs=[pl.BlockSpec((pairs, 2, 1, 16, 128), lambda j, i: (i, 0, j, 4, 0)),
                  pl.BlockSpec((pairs, 2, 1, 64, 128), lambda j, i: (i, 0, j, 0, 0))] + ([sums] if last else []),
        out_specs=pl.BlockSpec((8, 1, 512, 128), lambda j, i: (0, j, 0, 0)) if last else sums,
        out_shape=jax.ShapeDtypeStruct((8, 2, 512, 128), BF) if last else jax.ShapeDtypeStruct((2, 4096 // parts, 128 * parts), F32),
        scratch_shapes=[pltpu.VMEM((4096 // parts, 128 * parts), F32)] if last else [],
        compiler_params=pltpu.CompilerParams(vmem_limit_bytes=VMEM_BYTES),
        cost_estimate=pl.CostEstimate(flops=9 * 10**9, bytes_accessed=5 << 20, transcendentals=0),
        name="table_last" if last else "table_first",
    )(*([ids, bags] + ([start] if last else [])))


AXES = ("y", "zh", "x", "zl", "c")
HST = ("y", "zh", "x")
LOCAL = ("zl", "c")
SIZES = (4, 2, 4, 4, 2)
PLANE = ("y", "c", "x")


def weight_moves():
    up, down = [], []
    for d in range(256):
        y, zh, x, zl, c = (d // 64, d // 32 % 2, d // 8 % 4, d // 2 % 4, d % 2)
        unit = (zh * 4 + zl) * 16 + y * 4 + x
        up.append((d, (unit // 2) * 4 + 2 * c + unit % 2))
        down.append((d, c * 128 + unit))
    return up, down


def shards(pooled, cotangent, projection, w_up, w_down, w_compress, ln_gain, feature_map, bag_row_index):
    batch = pooled.shape[0] // 2
    scale = float(batch * 512) ** (-0.5)
    core = lax.axis_index("c").astype(jnp.int32).reshape(1)
    ids = jnp.transpose(bag_row_index, (1, 2, 0))
    swap = [(0, 1), (1, 0)]

    def layer(part):
        return layer_call(part, batch, feature_map, core, pooled, ids if part == 0 else None, cotangent,
                          projection.T, w_up, w_down, w_compress, ln_gain.reshape(1, 128), scale)

    def exchange(bag):
        return lax.all_to_all(bag, PLANE, 0, 0, tiled=True)

    bag0, keep0, send0, tail0 = layer(0)
    first = exchange(bag0)
    bag1, keep1, send1, tail1 = layer(1)
    acts = (keep0, lax.ppermute(send0, "c", swap), keep1, lax.ppermute(send1, "c", swap))
    weights = weight_call(acts, (tail0, tail1), scale)
    bag1, weights, first = lax.optimization_barrier((bag1, weights, first))
    weights = lax.psum_scatter(weights.reshape(8 * 336, 512), ("zh", "zl"), scatter_dimension=0, tiled=True)
    second = exchange(bag1)
    first = first.reshape(16, 2, 2, batch + 16, 128)
    rows = table_call(first, first)
    rows = table_call(first, second.reshape(16, 2, 2, batch, 128), rows)
    weights, _ = lax.optimization_barrier((weights, rows))
    rows = lax.psum_scatter(rows.reshape(8192, 128), ("zh", "zl"), scatter_dimension=0, tiled=True)
    pieces = jnp.concatenate(
        [weights[0:64].reshape(16, 4, 512),
         weights[64:320].reshape(8, 16, 2, 512).transpose(1, 0, 2, 3).reshape(16, 16, 512),
         jnp.broadcast_to(weights[320:328], (16, 8, 512))], axis=1)
    pieces = lax.all_to_all(pieces, ("y", "x"), 0, 0, tiled=True)
    total = jnp.sum(pieces.astype(F32), axis=0)
    up_moves, down_moves = weight_moves()
    gu = lax.ppermute(total[0:4], AXES, up_moves)
    gd = lax.ppermute(total[4:20], AXES, down_moves).reshape(8, 2, 512).transpose(1, 0, 2).reshape(2, 4096)
    tail = total[20:28].reshape(8, 4, 128).transpose(1, 0, 2).reshape(32, 128)
    tail = tail + lax.ppermute(tail, "c", swap)
    both = jnp.concatenate([tail[0:24, :64], tail[0:24, 64:]], axis=0)
    small = (both[32:48].T, both[0:32], tail[24])
    rows, gu, gd, small = lax.optimization_barrier((rows, gu, gd, small))
    table_grad = lax.ppermute(rows, ("zh", "c"), [(0, 0), (1, 2), (2, 1), (3, 3)]).astype(F32)
    return (table_grad.reshape(2, 512, 128), gu, gd) + tuple(small)


def solution(mesh):
    inner = Mesh(mesh.devices.reshape(SIZES), AXES)
    split = P(AXES, None, None)
    return jax.shard_map(
        shards,
        mesh=inner,
        in_specs=(split, split, P(), P(), P(), P(), P(), P(), split),
        out_specs=(P(HST, LOCAL, None), P(AXES, None), P(AXES, None), P(), P(), P()),
        check_vma=False,
    )
```

```python
import functools

import jax
import jax.numpy as jnp
from jax import lax
from jax.experimental import pallas as pl
from jax.experimental.pallas import tpu as pltpu
from jax.sharding import Mesh
from jax.sharding import PartitionSpec as P

BF, F32 = jnp.bfloat16, jnp.float32
VMEM_BYTES = 60 << 20


def dot_nn(a, b):
    return lax.dot_general(a, b, (((1,), (0,)), ((), ())), preferred_element_type=F32)


def dot_nt(a, b):
    return lax.dot_general(a, b, (((1,), (1,)), ((), ())), preferred_element_type=F32)


def dot_tn(a, b):
    return lax.dot_general(a, b, (((0,), (0,)), ((), ())), preferred_element_type=F32)


def out_norm(summed, cot, gain):
    centered = summed - jnp.mean(summed, axis=-1, keepdims=True)
    inverse = lax.rsqrt(jnp.mean(centered * centered, axis=-1, keepdims=True) + 1e-5)
    normed = centered * inverse
    cot_normed = cot * normed
    dnorm = cot * gain
    first = jnp.mean(dnorm, axis=-1, keepdims=True)
    second = jnp.mean(cot_normed * gain, axis=-1, keepdims=True)
    return inverse * (dnorm - first - normed * second), cot_normed


def fold8(v):
    return jnp.sum(v.reshape(v.shape[0] // 8, 8, 128), axis=0)


def layer_kernel(scale, b, part, with_ids, *refs):
    fm_ref, core_ref, pooled_ref = refs[:3]
    ids_ref = refs[3] if with_ids else None
    (cot_hbm, projt_ref, wup_hbm, wdown_hbm, wc_ref, gain_ref, bags_ref, keep_ref, send_ref, tail_ref,
     inv_ref, ds1, ds2, wups, wupr, cot_ref, wup_ref, wdown_ref, sems) = refs[3 + with_ids:]
    copies = [pltpu.make_async_copy(source, target, sems.at[i]) for i, (source, target) in enumerate((
        (wup_hbm, wup_ref), (wdown_hbm, wdown_ref), (cot_hbm.at[pl.ds(part * b, b)], cot_ref)))]
    for copy in copies:
        copy.start()
    for j in range(64):
        inv_ref[fm_ref[j]] = ((j // 16 * 4 + j // 2 % 4) * 2 + j // 8 % 2) * 2 + j % 2
    if with_ids:
        for n in range(64):
            v = ids_ref[n]
            rows = jnp.concatenate([jnp.bitwise_and(v, 255), lax.shift_right_logical(v, 8), jnp.zeros((12, 128), jnp.int32)], axis=0)
            bags_ref[inv_ref[n], 64:80, :] = rows.astype(F32).astype(BF)
    x = pooled_ref[...]
    gain = gain_ref[...]
    projt = projt_ref[...]
    wc = wc_ref[...]
    consts = jnp.transpose(jnp.concatenate([wc, projt], axis=0).astype(F32)).astype(BF)
    xcat = jnp.concatenate([x[s] for s in range(b)], axis=1)
    head = dot_nn(jnp.concatenate([projt, wc], axis=0), xcat)
    pts = [head[0:16, s * 128:(s + 1) * 128].astype(BF) for s in range(b)]
    inter = jnp.stack([dot_nt(pts[s], x[s]) for s in range(b)], axis=0)
    inter = jnp.swapaxes(inter, 0, 1)
    inter = jnp.concatenate([inter[k] for k in range(16)], axis=1)
    cen = inter - jnp.mean(inter, axis=1, keepdims=True)
    inv_fm = lax.rsqrt(jnp.mean(cen * cen, axis=1, keepdims=True) + 1e-5)
    normed = cen * inv_fm
    nb = normed.astype(BF)
    copies[0].wait()
    for q in range(4):
        wups[...] = wup_ref[:, q * 128:(q + 1) * 128].astype(F32)
        for k in range(16):
            wupr[k * 64:(k + 1) * 64, q * 128:(q + 1) * 128] = wups[pl.ds(k, 64, stride=16), :].astype(BF)
    preact = dot_nn(nb, wupr[...])
    sig = jax.nn.sigmoid(preact)
    hidden = (preact * sig).astype(BF)
    copies[1].wait()
    fm_out = dot_nn(hidden, wdown_ref[...])
    copies[2].wait()
    gg = jnp.zeros((8, 128), F32)
    dfms = []
    for m in range(32):
        if m % 16 == 0:
            xf = jnp.swapaxes(pooled_ref[:, m:m + 16, :], 0, 1)
            cf = jnp.swapaxes(cot_ref[:, m:m + 16, :], 0, 1)
        dsum, cot_normed = out_norm(
            fm_out[:, m * 128:(m + 1) * 128] + xf[m % 16].astype(F32), cf[m % 16].astype(F32), gain)
        gg += fold8(cot_normed)
        ds1[m] = dsum
        dfms.append(dsum.astype(BF))
    dlcs = []
    for s in range(b):
        dsum, cot_normed = out_norm(
            head[16:48, s * 128:(s + 1) * 128] + x[s, 32:64].astype(F32), cot_ref[s, 32:64, :].astype(F32), gain)
        gg += fold8(cot_normed)
        ds2[s] = dsum
        dlcs.append(dsum.astype(BF))
    dfm = jnp.concatenate(dfms, axis=1)
    hg = dot_nt(dfm, wdown_ref[...])
    dpre = (hg * sig * (1.0 + preact * (1.0 - sig))).astype(BF)
    first_core = core_ref[0] == 0
    for ref, flag in ((keep_ref, first_core), (send_ref, jnp.logical_not(first_core))):
        ref[:, 0:512] = jnp.where(flag, nb[:, 0:512], nb[:, 512:1024])
        ref[:, 512:1024] = dpre
        ref[:, 1024:1280] = jnp.where(flag, hidden[:, 0:256], hidden[:, 256:512])
        ref[:, 1280:5376] = dfm
    dnormed = dot_nt(dpre, wupr[...])
    first = jnp.mean(dnormed, axis=1, keepdims=True)
    second = jnp.mean(dnormed * normed, axis=1, keepdims=True)
    dinter = (inv_fm * (dnormed - first - normed * second)).astype(BF).astype(F32)
    dinter = jnp.swapaxes(jnp.stack([dinter[:, k * 64:(k + 1) * 64] for k in range(16)], axis=0), 0, 1)
    zero = jnp.zeros((16, 128), BF)
    tails = []
    for g in range(b // 16):
        outs = []
        for half in range(2):
            group = [g * 16 + half * 8 + i for i in range(8)]
            for s in group:
                dproj = dot_nn(dinter[s].astype(BF), x[s]).astype(BF)
                tails.append(jnp.concatenate([dlcs[s], dproj], axis=0))
            block = dinter[group[0]:group[0] + 8].reshape(128, 64)
            left = jnp.concatenate([jnp.transpose(block).astype(BF), consts], axis=1)
            right = jnp.concatenate(
                [jnp.concatenate([pts[s] if i == r else zero for i, s in enumerate(group)], axis=1) for r in range(8)]
                + [jnp.concatenate([tails[s] for s in group], axis=1)], axis=0)
            res = dot_nn(left, right)
            outs += [res[:, i * 128:(i + 1) * 128] for i in range(8)]
        for n in range(8):
            rows = [v[n * 8:(n + 1) * 8] for v in outs]
            if n >= 4:
                rows = [v + ds2[g * 16 + i, (n - 4) * 8:(n - 3) * 8, :] for i, v in enumerate(rows)]
            turned = jnp.swapaxes(jnp.stack(rows, axis=0), 0, 1)
            for i in range(8):
                v = turned[i]
                if n < 4:
                    v = v + ds1[n * 8 + i, g * 16:(g + 1) * 16, :]
                bags_ref[inv_ref[n * 8 + i], g * 16:(g + 1) * 16, :] = v.astype(BF)
    gsm = dot_nt(jnp.concatenate(tails, axis=1), xcat)
    tail_ref[...] = jnp.concatenate([
        jnp.concatenate([gsm[0:24], gsm[24:48]], axis=1),
        jnp.broadcast_to(jnp.sum(gg, axis=0, keepdims=True), (8, 128))], axis=0) * scale


def layer_call(part, batch, feature_map, core, pooled, ids, cotangent, projt, w_up, w_down, w_compress, gain, scale):
    full = lambda *sh: pl.BlockSpec(sh, lambda i: (0,) * len(sh))
    scalars = pl.BlockSpec(memory_space=pltpu.SMEM)
    far = pl.BlockSpec(memory_space=pl.ANY)
    with_ids = ids is not None
    depth = batch + 16 if with_ids else batch
    return pl.pallas_call(
        functools.partial(layer_kernel, scale, batch, part, int(with_ids)),
        grid=(1,),
        in_specs=[scalars, scalars, pl.BlockSpec((batch, 64, 128), lambda i: (part, 0, 0))]
        + ([full(64, 2, 128)] if with_ids else [])
        + [far, full(16, 64), far, far, full(32, 64), full(1, 128)],
        out_specs=[full(64, depth, 128), full(batch, 5376), full(batch, 5376), full(32, 128)],
        out_shape=[jax.ShapeDtypeStruct((64, depth, 128), BF),
                   jax.ShapeDtypeStruct((batch, 5376), BF),
                   jax.ShapeDtypeStruct((batch, 5376), BF),
                   jax.ShapeDtypeStruct((32, 128), F32)],
        scratch_shapes=[pltpu.SMEM((64,), jnp.int32),
                        pltpu.VMEM((32, batch, 128), F32), pltpu.VMEM((batch, 32, 128), F32),
                        pltpu.VMEM((1024, 128), F32), pltpu.VMEM((1024, 512), BF),
                        pltpu.VMEM((batch, 64, 128), BF), pltpu.VMEM((1024, 512), BF), pltpu.VMEM((512, 4096), BF),
                        pltpu.SemaphoreType.DMA((3,))],
        compiler_params=pltpu.CompilerParams(vmem_limit_bytes=VMEM_BYTES),
        cost_estimate=pl.CostEstimate(flops=15 * 10**9, bytes_accessed=10 << 20, transcendentals=0),
        name="layer_first" if with_ids else "layer_second",
    )(*([feature_map, core, pooled] + ([ids] if with_ids else [])
        + [cotangent, projt, w_up, w_down, w_compress, gain]))


def weight_kernel(scale, a0_ref, b0_ref, a1_ref, b1_ref, tail0_ref, tail1_ref, w_ref, gus):
    acts = jnp.concatenate([a0_ref[...], b0_ref[...], a1_ref[...], b1_ref[...]], axis=0)
    tail = tail0_ref[...] + tail1_ref[...]
    tail = jnp.concatenate([tail[q * 8:(q + 1) * 8, :] for q in range(4)], axis=1)
    tail = jnp.concatenate([tail, jnp.zeros((8, 512), F32)], axis=0).astype(BF)
    up = dot_tn(acts[:, 0:512], acts[:, 512:1024]) * scale
    for q in range(4):
        for k in range(8):
            gus[pl.ds(k, 64, stride=8), :] = up[k * 64:(k + 1) * 64, q * 128:(q + 1) * 128]
        for z in range(8):
            w_ref[z, 0:64, q * 128:(q + 1) * 128] = gus[z * 64:(z + 1) * 64, :].astype(BF)
    hid = acts[:, 1024:1280]
    for q in range(8):
        down = (dot_tn(hid, acts[:, 1280 + q * 512:1792 + q * 512]) * scale).astype(BF)
        for z in range(8):
            w_ref[z, 64 + q * 32:96 + q * 32, :] = down[z * 32:(z + 1) * 32, :]
    for z in range(8):
        w_ref[z, 320:336, :] = tail


def weight_call(acts, tails, scale):
    return pl.pallas_call(
        functools.partial(weight_kernel, scale),
        out_shape=jax.ShapeDtypeStruct((8, 336, 512), BF),
        scratch_shapes=[pltpu.VMEM((512, 128), F32)],
        compiler_params=pltpu.CompilerParams(vmem_limit_bytes=VMEM_BYTES),
        cost_estimate=pl.CostEstimate(flops=3 * 10**9, bytes_accessed=6 << 20, transcendentals=0),
        name="weight_grads",
    )(*acts, *tails)


def table_kernel(last, *refs):
    if last:
        core_ref, own_ids, other_ids, own_bags, other_bags, start_ref, out_ref, acc = refs
    else:
        core_ref, own_ids, other_ids, own_bags, other_bags, acc = refs
        acc = acc.at[0]
    side = slice(64, 128) if last else slice(0, 64)
    ids = []
    for ids_ref in (own_ids, other_ids):
        for i in range(8):
            codes = ids_ref[i, :, 0].astype(F32)
            codes = codes[:, 0:2] + 256.0 * codes[:, 2:4]
            ids.append(jnp.concatenate([codes[0][:, side], codes[1][:, side]], axis=1))
    ids = jnp.concatenate(ids, axis=0).astype(jnp.int32)
    low = jnp.transpose(lax.shift_right_logical(ids, 11).astype(F32), (1, 0))
    high = jnp.bitwise_and(lax.shift_right_logical(ids, 1), 512) + jnp.bitwise_and(ids, 511)
    mine = jnp.bitwise_and(lax.shift_right_logical(ids, 9), 1) == core_ref[0]
    high = jnp.where(mine, high, -1).astype(jnp.int16)
    iota = lax.broadcasted_iota(jnp.int16, (1024, 128), 0)
    for g in range(4):
        left, right = [], []
        for i in range(g * 4, (g + 1) * 4):
            values = (own_bags if i < 8 else other_bags)[i % 8, :, 0].reshape(128, 128)
            for t in range(2):
                r = 2 * i + t
                left.append(jnp.where(iota == high[r:r + 1, :], jnp.bfloat16(1), jnp.bfloat16(0)))
                column = jnp.broadcast_to(low[:, r:r + 1], (128, 128)).astype(BF)
                right.append(jnp.concatenate(
                    [jnp.where(column == jnp.bfloat16(q), values, jnp.bfloat16(0)) for q in range(2)], axis=1))
        part = jnp.dot(jnp.concatenate(left, axis=1), jnp.concatenate(right, axis=0), preferred_element_type=F32)
        if g == 0:
            acc[...] = start_ref[0] + part if last else part
        else:
            acc[...] += part
    if last:
        for block in range(4):
            h, q = block % 2, block // 2
            out_ref[0, block, 0] = acc[h * 512:(h + 1) * 512, q * 128:(q + 1) * 128].astype(BF)


def table_call(core, own_ids, other_ids, own, other, start=None):
    last = start is not None
    sums = pl.BlockSpec((1, 1024, 256), lambda j: (j, 0, 0))
    codes = pl.BlockSpec((8, 2, 1, 16, 128), lambda j: (0, 0, j, 4, 0))
    bags = pl.BlockSpec((8, 2, 1, 64, 128), lambda j: (0, 0, j, 0, 0))
    return pl.pallas_call(
        functools.partial(table_kernel, last),
        grid=(4,),
        in_specs=[pl.BlockSpec(memory_space=pltpu.SMEM), codes, codes, bags, bags] + ([sums] if last else []),
        out_specs=pl.BlockSpec((1, 4, 1, 512, 128), lambda j: (j // 2, 0, j % 2, 0, 0)) if last else sums,
        out_shape=jax.ShapeDtypeStruct((2, 4, 2, 512, 128), BF) if last else jax.ShapeDtypeStruct((4, 1024, 256), F32),
        scratch_shapes=[pltpu.VMEM((1024, 256), F32)] if last else [],
        compiler_params=pltpu.CompilerParams(vmem_limit_bytes=VMEM_BYTES),
        cost_estimate=pl.CostEstimate(flops=9 * 10**9, bytes_accessed=5 << 20, transcendentals=0),
        name="table_last" if last else "table_first",
    )(*([core, own_ids, other_ids, own, other] + ([start] if last else [])))


AXES = ("y", "zh", "x", "zl", "c")
HST = ("y", "zh", "x")
LOCAL = ("zl", "c")
SIZES = (4, 2, 4, 4, 2)


def weight_moves():
    up, down = [], []
    for d in range(256):
        y, zh, x, zl, c = (d // 64, d // 32 % 2, d // 8 % 4, d // 2 % 4, d % 2)
        unit = (zh * 4 + zl) * 16 + y * 4 + x
        up.append((d, (unit // 2) * 4 + 2 * c + unit % 2))
        down.append((d, c * 128 + unit))
    return up, down


def shards(pooled, cotangent, projection, w_up, w_down, w_compress, ln_gain, feature_map, bag_row_index):
    batch = pooled.shape[0] // 2
    scale = float(batch * 512) ** (-0.5)
    core = lax.axis_index("c").astype(jnp.int32).reshape(1)
    ids = jnp.transpose(bag_row_index, (1, 2, 0))
    swap = [(0, 1), (1, 0)]

    def layer(part):
        return layer_call(part, batch, feature_map, core, pooled, ids if part == 0 else None, cotangent,
                          projection.T, w_up, w_down, w_compress, ln_gain.reshape(1, 128), scale)

    def exchange(bag):
        return lax.all_to_all(bag, ("y", "x"), 0, 0, tiled=True)

    bag0, keep0, send0, tail0 = layer(0)
    first = exchange(bag0)
    bag1, keep1, send1, tail1 = layer(1)
    acts = (keep0, lax.ppermute(send0, "c", swap), keep1, lax.ppermute(send1, "c", swap))
    weights = weight_call(acts, (tail0, tail1), scale)
    bag1, weights, first = lax.optimization_barrier((bag1, weights, first))
    weights = lax.psum_scatter(weights.reshape(8 * 336, 512), ("zh", "zl"), scatter_dimension=0, tiled=True)
    second = exchange(bag1)
    first = first.reshape(8, 2, 4, batch + 16, 128)
    other = lax.ppermute(first, "c", swap)
    rows = table_call(core, first, other, first, other)
    second, rows = lax.optimization_barrier((second, rows))
    second = second.reshape(8, 2, 4, batch, 128)
    rows = table_call(core, first, other, second, lax.ppermute(second, "c", swap), rows)
    weights, _ = lax.optimization_barrier((weights, rows))
    rows = lax.psum_scatter(rows.reshape(8192, 128), ("zh", "zl"), scatter_dimension=0, tiled=True)
    pieces = jnp.concatenate(
        [weights[0:64].reshape(16, 4, 512),
         weights[64:320].reshape(8, 16, 2, 512).transpose(1, 0, 2, 3).reshape(16, 16, 512),
         jnp.broadcast_to(weights[320:328], (16, 8, 512))], axis=1)
    pieces = lax.all_to_all(pieces, ("y", "x"), 0, 0, tiled=True)
    total = jnp.sum(pieces.astype(F32), axis=0)
    up_moves, down_moves = weight_moves()
    gu = lax.ppermute(total[0:4], AXES, up_moves)
    gd = lax.ppermute(total[4:20], AXES, down_moves).reshape(8, 2, 512).transpose(1, 0, 2).reshape(2, 4096)
    tail = total[20:28].reshape(8, 4, 128).transpose(1, 0, 2).reshape(32, 128)
    tail = tail + lax.ppermute(tail, "c", swap)
    both = jnp.concatenate([tail[0:24, :64], tail[0:24, 64:]], axis=0)
    small = (both[32:48].T, both[0:32], tail[24])
    rows, gu, gd, small = lax.optimization_barrier((rows, gu, gd, small))
    return (rows.astype(F32).reshape(2, 512, 128), gu, gd) + tuple(small)


def solution(mesh):
    inner = Mesh(mesh.devices.reshape(SIZES), AXES)
    split = P(AXES, None, None)
    return jax.shard_map(
        shards,
        mesh=inner,
        in_specs=(split, split, P(), P(), P(), P(), P(), P(), split),
        out_specs=(P(HST, LOCAL, None), P(AXES, None), P(AXES, None), P(), P(), P()),
        check_vma=False,
    )
```

```python
import functools

import jax
import jax.numpy as jnp
from jax import lax
from jax.experimental import pallas as pl
from jax.experimental.pallas import tpu as pltpu
from jax.sharding import Mesh
from jax.sharding import PartitionSpec as P

BF, F32 = jnp.bfloat16, jnp.float32
VMEM_BYTES = 60 << 20


def dot_nn(a, b):
    return lax.dot_general(a, b, (((1,), (0,)), ((), ())), preferred_element_type=F32)


def dot_nt(a, b):
    return lax.dot_general(a, b, (((1,), (1,)), ((), ())), preferred_element_type=F32)


def dot_tn(a, b):
    return lax.dot_general(a, b, (((0,), (0,)), ((), ())), preferred_element_type=F32)


def out_norm(summed, cot, gain):
    centered = summed - jnp.mean(summed, axis=-1, keepdims=True)
    inverse = lax.rsqrt(jnp.mean(centered * centered, axis=-1, keepdims=True) + 1e-5)
    normed = centered * inverse
    cot_normed = cot * normed
    dnorm = cot * gain
    first = jnp.mean(dnorm, axis=-1, keepdims=True)
    second = jnp.mean(cot_normed * gain, axis=-1, keepdims=True)
    return inverse * (dnorm - first - normed * second), cot_normed


def fold8(v):
    return jnp.sum(v.reshape(v.shape[0] // 8, 8, 128), axis=0)


def layer_kernel(scale, b, part, with_ids, *refs):
    fm_ref, core_ref, pooled_ref = refs[:3]
    ids_ref = refs[3] if with_ids else None
    (cot_hbm, projt_ref, wup_hbm, wdown_hbm, wc_ref, gain_ref, bags_ref, keep_ref, send_ref, tail_ref,
     inv_ref, ds1, ds2, wupr, cot_ref, wup_ref, wdown_ref, sems) = refs[3 + with_ids:]
    copies = [pltpu.make_async_copy(source, target, sems.at[i]) for i, (source, target) in enumerate((
        (wup_hbm, wup_ref), (wdown_hbm, wdown_ref), (cot_hbm.at[pl.ds(part * b, b)], cot_ref)))]
    for copy in copies:
        copy.start()
    for j in range(64):
        inv_ref[fm_ref[j]] = ((j // 16 * 4 + j // 2 % 4) * 2 + j // 8 % 2) * 2 + j % 2
    if with_ids:
        for n in range(64):
            v = ids_ref[n]
            rows = jnp.concatenate([jnp.bitwise_and(v, 255), lax.shift_right_logical(v, 8), jnp.zeros((12, 128), jnp.int32)], axis=0)
            bags_ref[inv_ref[n], 64:80, :] = rows.astype(F32).astype(BF)
    x = pooled_ref[...]
    gain = gain_ref[...]
    projt = projt_ref[...]
    wc = wc_ref[...]
    consts = jnp.transpose(jnp.concatenate([wc, projt], axis=0).astype(F32)).astype(BF)
    xcat = jnp.concatenate([x[s] for s in range(b)], axis=1)
    head = dot_nn(jnp.concatenate([projt, wc], axis=0), xcat)
    pts = [head[0:16, s * 128:(s + 1) * 128].astype(BF) for s in range(b)]
    inter = jnp.stack([dot_nt(pts[s], x[s]) for s in range(b)], axis=0)
    inter = jnp.swapaxes(inter, 0, 1)
    inter = jnp.concatenate([inter[k] for k in range(16)], axis=1)
    cen = inter - jnp.mean(inter, axis=1, keepdims=True)
    inv_fm = lax.rsqrt(jnp.mean(cen * cen, axis=1, keepdims=True) + 1e-5)
    normed = cen * inv_fm
    nb = normed.astype(BF)
    copies[0].wait()
    for q in range(4):
        for n in range(4):
            turned = jnp.swapaxes(wup_ref[n * 256:(n + 1) * 256, q * 128:(q + 1) * 128].reshape(16, 16, 128), 0, 1)
            for k in range(16):
                wupr[k * 64 + n * 16:k * 64 + n * 16 + 16, q * 128:(q + 1) * 128] = turned[k]
    preact = dot_nn(nb, wupr[...])
    sig = jax.nn.sigmoid(preact)
    hidden = (preact * sig).astype(BF)
    copies[1].wait()
    fm_out = dot_nn(hidden, wdown_ref[...])
    copies[2].wait()
    gg = jnp.zeros((8, 128), F32)
    dfms = []
    for m in range(32):
        if m % 16 == 0:
            xf = jnp.swapaxes(pooled_ref[:, m:m + 16, :], 0, 1)
            cf = jnp.swapaxes(cot_ref[:, m:m + 16, :], 0, 1)
        dsum, cot_normed = out_norm(
            fm_out[:, m * 128:(m + 1) * 128] + xf[m % 16].astype(F32), cf[m % 16].astype(F32), gain)
        gg += fold8(cot_normed)
        ds1[m] = dsum
        dfms.append(dsum.astype(BF))
    dlcs = []
    for s in range(b):
        dsum, cot_normed = out_norm(
            head[16:48, s * 128:(s + 1) * 128] + x[s, 32:64].astype(F32), cot_ref[s, 32:64, :].astype(F32), gain)
        gg += fold8(cot_normed)
        ds2[s] = dsum
        dlcs.append(dsum.astype(BF))
    dfm = jnp.concatenate(dfms, axis=1)
    hg = dot_nt(dfm, wdown_ref[...])
    dpre = (hg * sig * (1.0 + preact * (1.0 - sig))).astype(BF)
    first_core = core_ref[0] == 0
    for ref, flag in ((keep_ref, first_core), (send_ref, jnp.logical_not(first_core))):
        ref[:, 0:512] = jnp.where(flag, nb[:, 0:512], nb[:, 512:1024])
        ref[:, 512:1024] = dpre
        ref[:, 1024:1280] = jnp.where(flag, hidden[:, 0:256], hidden[:, 256:512])
        ref[:, 1280:5376] = dfm
    dnormed = dot_nt(dpre, wupr[...])
    first = jnp.mean(dnormed, axis=1, keepdims=True)
    second = jnp.mean(dnormed * normed, axis=1, keepdims=True)
    dinter = (inv_fm * (dnormed - first - normed * second)).astype(BF).astype(F32)
    dinter = jnp.swapaxes(jnp.stack([dinter[:, k * 64:(k + 1) * 64] for k in range(16)], axis=0), 0, 1)
    zero = jnp.zeros((16, 128), BF)
    tails = []
    for g in range(b // 16):
        outs = []
        for half in range(2):
            group = [g * 16 + half * 8 + i for i in range(8)]
            for s in group:
                dproj = dot_nn(dinter[s].astype(BF), x[s]).astype(BF)
                tails.append(jnp.concatenate([dlcs[s], dproj], axis=0))
            block = dinter[group[0]:group[0] + 8].reshape(128, 64)
            left = jnp.concatenate([jnp.transpose(block).astype(BF), consts], axis=1)
            right = jnp.concatenate(
                [jnp.concatenate([pts[s] if i == r else zero for i, s in enumerate(group)], axis=1) for r in range(8)]
                + [jnp.concatenate([tails[s] for s in group], axis=1)], axis=0)
            res = dot_nn(left, right)
            outs += [res[:, i * 128:(i + 1) * 128] for i in range(8)]
        for n in range(8):
            rows = [v[n * 8:(n + 1) * 8] for v in outs]
            if n >= 4:
                rows = [v + ds2[g * 16 + i, (n - 4) * 8:(n - 3) * 8, :] for i, v in enumerate(rows)]
            turned = jnp.swapaxes(jnp.stack(rows, axis=0), 0, 1)
            for i in range(8):
                v = turned[i]
                if n < 4:
                    v = v + ds1[n * 8 + i, g * 16:(g + 1) * 16, :]
                bags_ref[inv_ref[n * 8 + i], g * 16:(g + 1) * 16, :] = v.astype(BF)
    gsm = dot_nt(jnp.concatenate(tails, axis=1), xcat)
    tail_ref[...] = jnp.concatenate([
        jnp.concatenate([gsm[0:24], gsm[24:48]], axis=1),
        jnp.broadcast_to(jnp.sum(gg, axis=0, keepdims=True), (8, 128))], axis=0) * scale


def layer_call(part, batch, feature_map, core, pooled, ids, cotangent, projt, w_up, w_down, w_compress, gain, scale):
    full = lambda *sh: pl.BlockSpec(sh, lambda i: (0,) * len(sh))
    scalars = pl.BlockSpec(memory_space=pltpu.SMEM)
    far = pl.BlockSpec(memory_space=pl.ANY)
    with_ids = ids is not None
    depth = batch + 16 if with_ids else batch
    return pl.pallas_call(
        functools.partial(layer_kernel, scale, batch, part, int(with_ids)),
        grid=(1,),
        in_specs=[scalars, scalars, pl.BlockSpec((batch, 64, 128), lambda i: (part, 0, 0))]
        + ([full(64, 2, 128)] if with_ids else [])
        + [far, full(16, 64), far, far, full(32, 64), full(1, 128)],
        out_specs=[full(64, depth, 128), full(batch, 5376), full(batch, 5376), full(32, 128)],
        out_shape=[jax.ShapeDtypeStruct((64, depth, 128), BF),
                   jax.ShapeDtypeStruct((batch, 5376), BF),
                   jax.ShapeDtypeStruct((batch, 5376), BF),
                   jax.ShapeDtypeStruct((32, 128), F32)],
        scratch_shapes=[pltpu.SMEM((64,), jnp.int32),
                        pltpu.VMEM((32, batch, 128), F32), pltpu.VMEM((batch, 32, 128), F32),
                        pltpu.VMEM((1024, 512), BF),
                        pltpu.VMEM((batch, 64, 128), BF), pltpu.VMEM((1024, 512), BF), pltpu.VMEM((512, 4096), BF),
                        pltpu.SemaphoreType.DMA((3,))],
        compiler_params=pltpu.CompilerParams(vmem_limit_bytes=VMEM_BYTES),
        cost_estimate=pl.CostEstimate(flops=15 * 10**9, bytes_accessed=10 << 20, transcendentals=0),
        name="layer_first" if with_ids else "layer_second",
    )(*([feature_map, core, pooled] + ([ids] if with_ids else [])
        + [cotangent, projt, w_up, w_down, w_compress, gain]))


def weight_kernel(scale, a0_ref, b0_ref, a1_ref, b1_ref, tail0_ref, tail1_ref, w_ref):
    acts = jnp.concatenate([a0_ref[...], b0_ref[...], a1_ref[...], b1_ref[...]], axis=0)
    tail = tail0_ref[...] + tail1_ref[...]
    tail = jnp.concatenate([tail[q * 8:(q + 1) * 8, :] for q in range(4)], axis=1)
    tail = jnp.concatenate([tail, jnp.zeros((8, 512), F32)], axis=0).astype(BF)
    up = dot_tn(acts[:, 0:512], acts[:, 512:1024]) * scale
    for q in range(4):
        for z in range(8):
            turned = jnp.swapaxes(jnp.stack(
                [up[k * 64 + z * 8:k * 64 + z * 8 + 8, q * 128:(q + 1) * 128] for k in range(8)], axis=0), 0, 1)
            w_ref[z, 0:64, q * 128:(q + 1) * 128] = turned.reshape(64, 128).astype(BF)
    hid = acts[:, 1024:1280]
    for q in range(8):
        down = (dot_tn(hid, acts[:, 1280 + q * 512:1792 + q * 512]) * scale).astype(BF)
        for z in range(8):
            w_ref[z, 64 + q * 32:96 + q * 32, :] = down[z * 32:(z + 1) * 32, :]
    for z in range(8):
        w_ref[z, 320:336, :] = tail


def weight_call(acts, tails, scale):
    return pl.pallas_call(
        functools.partial(weight_kernel, scale),
        out_shape=jax.ShapeDtypeStruct((8, 336, 512), BF),
        compiler_params=pltpu.CompilerParams(vmem_limit_bytes=24 << 20),
        cost_estimate=pl.CostEstimate(flops=3 * 10**9, bytes_accessed=6 << 20, transcendentals=0),
        name="weight_grads",
    )(*acts, *tails)


def table_kernel(last, *refs):
    if last:
        core_ref, own_ids, other_ids, own_bags, other_bags, start_ref, out_ref, acc = refs
    else:
        core_ref, own_ids, other_ids, own_bags, other_bags, acc = refs
        acc = acc.at[0]
    side = slice(64, 128) if last else slice(0, 64)
    ids = []
    for ids_ref in (own_ids, other_ids):
        for i in range(8):
            codes = ids_ref[i, :, 0].astype(F32)
            codes = codes[:, 0:2] + 256.0 * codes[:, 2:4]
            ids.append(jnp.concatenate([codes[0][:, side], codes[1][:, side]], axis=1))
    ids = jnp.concatenate(ids, axis=0).astype(jnp.int32)
    low = jnp.transpose(lax.shift_right_logical(ids, 11).astype(F32), (1, 0))
    high = jnp.bitwise_and(lax.shift_right_logical(ids, 1), 512) + jnp.bitwise_and(ids, 511)
    mine = jnp.bitwise_and(lax.shift_right_logical(ids, 9), 1) == core_ref[0]
    high = jnp.where(mine, high, -1).astype(jnp.int16)
    iota = lax.broadcasted_iota(jnp.int16, (1024, 128), 0)
    for g in range(4):
        left, right = [], []
        for i in range(g * 4, (g + 1) * 4):
            values = (own_bags if i < 8 else other_bags)[i % 8, :, 0].reshape(128, 128)
            for t in range(2):
                r = 2 * i + t
                left.append(jnp.where(iota == high[r:r + 1, :], jnp.bfloat16(1), jnp.bfloat16(0)))
                column = jnp.broadcast_to(low[:, r:r + 1], (128, 128)).astype(BF)
                right.append(jnp.concatenate(
                    [jnp.where(column == jnp.bfloat16(q), values, jnp.bfloat16(0)) for q in range(2)], axis=1))
        part = jnp.dot(jnp.concatenate(left, axis=1), jnp.concatenate(right, axis=0), preferred_element_type=F32)
        if g == 0:
            acc[...] = start_ref[0] + part if last else part
        else:
            acc[...] += part
    if last:
        for block in range(4):
            h, q = block % 2, block // 2
            out_ref[0, block, 0] = acc[h * 512:(h + 1) * 512, q * 128:(q + 1) * 128].astype(BF)


def table_call(core, own_ids, other_ids, own, other, start=None):
    last = start is not None
    sums = pl.BlockSpec((1, 1024, 256), lambda j: (j, 0, 0))
    codes = pl.BlockSpec((8, 2, 1, 16, 128), lambda j: (0, 0, j, 4, 0))
    bags = pl.BlockSpec((8, 2, 1, 64, 128), lambda j: (0, 0, j, 0, 0))
    return pl.pallas_call(
        functools.partial(table_kernel, last),
        grid=(4,),
        in_specs=[pl.BlockSpec(memory_space=pltpu.SMEM), codes, codes, bags, bags] + ([sums] if last else []),
        out_specs=pl.BlockSpec((1, 4, 1, 512, 128), lambda j: (j // 2, 0, j % 2, 0, 0)) if last else sums,
        out_shape=jax.ShapeDtypeStruct((2, 4, 2, 512, 128), BF) if last else jax.ShapeDtypeStruct((4, 1024, 256), F32),
        scratch_shapes=[pltpu.VMEM((1024, 256), F32)] if last else [],
        compiler_params=pltpu.CompilerParams(vmem_limit_bytes=32 << 20),
        cost_estimate=pl.CostEstimate(flops=9 * 10**9, bytes_accessed=5 << 20, transcendentals=0),
        name="table_last" if last else "table_first",
    )(*([core, own_ids, other_ids, own, other] + ([start] if last else [])))


AXES = ("y", "zh", "x", "zl", "c")
HST = ("y", "zh", "x")
LOCAL = ("zl", "c")
SIZES = (4, 2, 4, 4, 2)


def weight_moves():
    up, down = [], []
    for d in range(256):
        y, zh, x, zl, c = (d // 64, d // 32 % 2, d // 8 % 4, d // 2 % 4, d % 2)
        unit = (zh * 4 + zl) * 16 + y * 4 + x
        up.append((d, (unit // 2) * 4 + 2 * c + unit % 2))
        down.append((d, c * 128 + unit))
    return up, down


def shards(pooled, cotangent, projection, w_up, w_down, w_compress, ln_gain, feature_map, bag_row_index):
    batch = pooled.shape[0] // 2
    scale = float(batch * 512) ** (-0.5)
    core = lax.axis_index("c").astype(jnp.int32).reshape(1)
    ids = jnp.transpose(bag_row_index, (1, 2, 0))
    swap = [(0, 1), (1, 0)]

    def layer(part):
        return layer_call(part, batch, feature_map, core, pooled, ids if part == 0 else None, cotangent,
                          projection.T, w_up, w_down, w_compress, ln_gain.reshape(1, 128), scale)

    def exchange(bag):
        return lax.all_to_all(bag, ("y", "x"), 0, 0, tiled=True)

    bag0, keep0, send0, tail0 = layer(0)
    first = exchange(bag0)
    bag1, keep1, send1, tail1 = layer(1)
    acts = (keep0, lax.ppermute(send0, "c", swap), keep1, lax.ppermute(send1, "c", swap))
    weights = weight_call(acts, (tail0, tail1), scale)
    bag1, weights, first = lax.optimization_barrier((bag1, weights, first))
    weights = lax.psum_scatter(weights.reshape(8 * 336, 512), ("zh", "zl"), scatter_dimension=0, tiled=True)
    second = exchange(bag1)
    first = first.reshape(8, 2, 4, batch + 16, 128)
    other = lax.ppermute(first, "c", swap)
    rows = table_call(core, first, other, first, other)
    second, rows = lax.optimization_barrier((second, rows))
    second = second.reshape(8, 2, 4, batch, 128)
    rows = table_call(core, first, other, second, lax.ppermute(second, "c", swap), rows)
    weights, _ = lax.optimization_barrier((weights, rows))
    rows = lax.psum_scatter(rows.reshape(8192, 128), ("zh", "zl"), scatter_dimension=0, tiled=True)
    pieces = jnp.concatenate(
        [weights[0:64].reshape(16, 4, 512),
         weights[64:320].reshape(8, 16, 2, 512).transpose(1, 0, 2, 3).reshape(16, 16, 512),
         jnp.broadcast_to(weights[320:328], (16, 8, 512))], axis=1)
    pieces = lax.all_to_all(pieces, ("y", "x"), 0, 0, tiled=True)
    total = jnp.sum(pieces.astype(F32), axis=0)
    up_moves, down_moves = weight_moves()
    gu = lax.ppermute(total[0:4], AXES, up_moves)
    gd = lax.ppermute(total[4:20], AXES, down_moves).reshape(8, 2, 512).transpose(1, 0, 2).reshape(2, 4096)
    tail = total[20:28].reshape(8, 4, 128).transpose(1, 0, 2).reshape(32, 128)
    tail = tail + lax.ppermute(tail, "c", swap)
    both = jnp.concatenate([tail[0:24, :64], tail[0:24, 64:]], axis=0)
    small = (both[32:48].T, both[0:32], tail[24])
    rows, gu, gd, small = lax.optimization_barrier((rows, gu, gd, small))
    return (rows.astype(F32).reshape(2, 512, 128), gu, gd) + tuple(small)


def solution(mesh):
    inner = Mesh(mesh.devices.reshape(SIZES), AXES)
    split = P(AXES, None, None)
    return jax.shard_map(
        shards,
        mesh=inner,
        in_specs=(split, split, P(), P(), P(), P(), P(), P(), split),
        out_specs=(P(HST, LOCAL, None), P(AXES, None), P(AXES, None), P(), P(), P()),
        check_vma=False,
    )
```
